32 devices in a mesh: grp: 2 (over x), pulse: 16 (over z, y, core).
Axes of the slice: x: 2, y: 2, z: 4, core: 2. Of those that a mesh axis runs over, the one named last changes fastest.
Arguments:
- echo: float32 [2, 4, 4, 2048, 1024], P(None, 'grp', None, 'pulse'), parts along dimension 1, may hold values from -6 to 6
- spectral_shift_units: int32 [1024], replicated, may hold values from -256 to 256
Outputs:
- doppler: float32 [2, 4, 4, 1024, 2048], P(None, 'grp', None, 'pulse'), parts along dimension 1
The draws below stay inside these ranges and needn't reach their ends.
There are 2 independent parts, one for each index of `grp`. The reference program is written for one: setup_inputs(seed, part) draws one part's arguments, and reference() takes and returns one part's arrays. A program takes and returns all parts, laid end to end along the dimension named above; an argument that names none is the same for every part. Nothing has to cross between parts.
Inputs may be any that keep to these rules, and one draw needn't show every extreme that they name: `spectral_shift_units`: bin codes may repeat.
All inputs are finite; a program needn't handle non-finite values.
Results may differ from the reference program's by a relative error of at most 0.00007.
Values sent between devices are 32-bit elements; how exact they have to be, the bound alone decides.
No kernel may reach another device: no remote copies, remote signals or barrier semaphores. Data moves between devices by JAX's collectives and lax.ppermute only.
A program may use at most 192 MiB of HBM per device.

```python
import math
import jax
import jax.numpy as jnp

PULSES = 2048
BINS = 1024
CH = 4
CPIS = 2


def plant(result, stream_key, smallest, largest):
    spot = [jax.random.randint(jax.random.fold_in(stream_key, axis), (), 0, length) for axis, length in enumerate(result.shape)]
    longest = result.shape.index(max(result.shape))
    neighbour = spot[:longest] + [(spot[longest] + 1) % result.shape[longest]] + spot[longest + 1:]
    return result.at[tuple(spot)].set(smallest).at[tuple(neighbour)].set(largest)


def shard_levels(own_key, extent, split, least, largest):
    gain, own = 1.0, jax.random.fold_in(own_key, 6)
    for axis_at, parts in split:
        draws = jnp.exp(jax.random.uniform(jax.random.fold_in(own, axis_at), (parts,), jnp.float32, least / len(split), largest / len(split)))
        gain = gain * jnp.repeat(draws, extent[axis_at] // parts).reshape([-1 if axis == axis_at else 1 for axis in range(len(extent))])
    return gain


def normal_values(own_key, shape, width, limit, shards=(), kind=jnp.bfloat16):
    array = width * jax.random.normal(own_key, shape, jnp.float32)
    if shards:
        array = array * shard_levels(own_key, shape, shards, -0.22, 0.18)
    return jnp.clip(array, -limit, limit).astype(kind)


def setup_inputs(seed: int = 0, part: int = 0) -> dict:
    key_list = jax.random.split(jax.random.key(seed), 3)
    part_splits = jax.random.split(jax.random.fold_in(key_list[2], part), 3)
    return {
        "echo": normal_values(part_splits[0], (2, CPIS, CH, PULSES, BINS), 1.0, 6.0, ((3, 16),), jnp.float32),
        "spectral_shift_units": plant(jax.random.randint(key_list[1], (BINS,), -(PULSES // 8), PULSES // 8 + 1), jax.random.fold_in(key_list[1], 1), -(PULSES // 8), (PULSES // 8 + 1) - 1).astype(jnp.int32),
    }


BETA_KB = math.pi * math.sqrt(35.2)

def bessel_zero(value):
    quarter = value * value * 0.25
    term = jnp.ones_like(value)
    total = jnp.ones_like(value)
    for order in range(1, 41):
        term = term * quarter / float(order * order)
        total = total + term
    return total

def kernel(distance):
    ratio = distance / 4.0
    inner = jnp.maximum(1.0 - ratio * ratio, 0.0)
    peak = bessel_zero(BETA_KB * jnp.ones((), distance.dtype))
    return bessel_zero(BETA_KB * jnp.sqrt(inner)) / peak

def positions(spectral_shift_units, echo_numbers, number_of_echoes):
    center_tone_hertz = 16 * number_of_echoes
    quotient_numerator = 2 * (echo_numbers[None, :] - number_of_echoes // 2) * center_tone_hertz
    quotient_denominator = center_tone_hertz + spectral_shift_units[:, None]
    cell_floor = jnp.floor_divide(quotient_numerator, quotient_denominator)
    fraction = (quotient_numerator - cell_floor * quotient_denominator).astype(jnp.float32) / quotient_denominator.astype(jnp.float32)
    return (cell_floor, fraction)

def correction(number_of_echoes):
    grid_size = 2 * number_of_echoes
    doppler_bin_index = jnp.arange(number_of_echoes, dtype=jnp.int32) - number_of_echoes // 2
    phase = math.pi * 8.0 / grid_size * doppler_bin_index.astype(jnp.float32)
    root = jnp.sqrt(BETA_KB * BETA_KB - phase * phase)
    parity = (1 - 2 * (doppler_bin_index % 2)).astype(jnp.float32)
    peak = bessel_zero(BETA_KB * jnp.ones((), jnp.float32))
    return parity * peak * root / (8.0 * jnp.sinh(root)) / math.sqrt(number_of_echoes)

def reference(echo, spectral_shift_units):
    number_of_echoes = PULSES
    grid_size = 2 * number_of_echoes
    cell_floor, fraction = positions(spectral_shift_units, jnp.arange(number_of_echoes, dtype=jnp.int32), number_of_echoes)
    samples = jnp.swapaxes(echo, 3, 4)
    bin_rows = jnp.broadcast_to(jnp.arange(BINS, dtype=jnp.int32)[:, None], cell_floor.shape)
    gridded = jnp.zeros(samples.shape[:4] + (grid_size,), jnp.float32)
    for tap_index in range(8):
        cell_ids = (cell_floor + (number_of_echoes + tap_index - 3)) % grid_size
        weight = kernel(tap_index - 3 - fraction)
        gridded = gridded.at[:, :, :, bin_rows, cell_ids].add(samples * weight)
    spectrum = jnp.fft.fft(gridded[0] + 1j * gridded[1], axis=-1)
    half_count = number_of_echoes // 2
    picked = jnp.concatenate([spectrum[..., grid_size - half_count:], spectrum[..., :half_count]], axis=-1)
    scaling = correction(number_of_echoes)
    return jnp.stack([jnp.real(picked) * scaling, jnp.imag(picked) * scaling]).astype(jnp.float32)
```

```python
import functools
import math

import jax
import jax.numpy as jnp
import numpy as np
from jax import lax
from jax.experimental import pallas as pl
from jax.experimental.pallas import tpu as pltpu
from jax.sharding import PartitionSpec as P

PULSES = 2048
BINS = 1024
TONE = 16 * PULSES
CODE_MAX = PULSES // 8
MINOR = 16
MAJOR = PULSES // MINOR
PAD = 10
BLOCKS = MAJOR // 8
LANES = 128

BETA_KB = math.pi * math.sqrt(35.2)


def bessel_zero(value):
    quarter = value * value * 0.25
    term = jnp.ones_like(value)
    total = jnp.ones_like(value)
    for order in range(1, 41):
        term = term * quarter / float(order * order)
        total = total + term
    return total


def correction(number_of_echoes):
    grid_size = 2 * number_of_echoes
    doppler_bin_index = jnp.arange(number_of_echoes, dtype=jnp.int32) - number_of_echoes // 2
    phase = math.pi * 8.0 / grid_size * doppler_bin_index.astype(jnp.float32)
    root = jnp.sqrt(BETA_KB * BETA_KB - phase * phase)
    parity = (1 - 2 * (doppler_bin_index % 2)).astype(jnp.float32)
    peak = bessel_zero(BETA_KB * jnp.ones((), jnp.float32))
    return parity * peak * root / (8.0 * jnp.sinh(root)) / math.sqrt(number_of_echoes)


@functools.lru_cache(None)
def windows():
    pulse = np.arange(PULSES)
    numerator = 2 * (pulse - PULSES // 2) * TONE
    ends = np.stack([numerator // (TONE + code) - 2 * (pulse - PULSES // 2) for code in (-CODE_MAX, CODE_MAX)])
    low, high = ends.min(0) - 3, ends.max(0) + 4
    out, start = [], 0
    for block in range(BLOCKS):
        row = []
        pairs = np.arange(128 * block, 128 * (block + 1))
        for parity in range(2):
            offsets = []
            for e in range(-PAD, PAD + 1):
                source = (pairs - e) % PULSES
                reach = 2 * e + parity
                if np.any((low[source] <= reach) & (reach <= high[source])):
                    offsets.append(e)
            row.append((start, tuple(offsets)))
            start += len(offsets)
        out.append(tuple(row))
    return tuple(out), start


@functools.lru_cache(None)
def series():
    terms = [1.0]
    for order in range(1, 41):
        terms.append(terms[-1] * (BETA_KB * BETA_KB / 4.0) / float(order * order))
    peak = math.fsum(terms)
    return tuple(term / peak for term in terms)


@functools.lru_cache(None)
def turns():
    r = np.arange(2 * MINOR)[:, None, None]
    n2 = np.arange(MAJOR)[None, :, None]
    q2 = np.arange(MAJOR)[None, None, :]
    angle = 2.0 * math.pi / (2 * PULSES) * ((32 * q2 + r) * n2 % (2 * PULSES))
    cosine, sine = np.cos(angle), np.sin(angle)
    full = np.concatenate(
        [np.concatenate([cosine, sine], 2), np.concatenate([-sine, cosine], 2)], 1
    )
    high = full.astype(jnp.bfloat16)
    low = (full - high.astype(np.float64)).astype(jnp.bfloat16)
    both = np.stack([high, low], 1)
    return both.reshape(MINOR, 2, 2, 2 * MAJOR, 2 * MAJOR)


def pack_body(rows, bins, echo_ref, out_ref):
    depth = echo_ref.shape[2] // MINOR
    lane = lax.broadcasted_iota(jnp.int32, (depth, LANES), 1) // bins
    for part in range(2):
        for m1 in range(MINOR):
            taken = [echo_ref[part, row, pl.ds(m1, depth, stride=MINOR), :] for row in range(rows)]
            for dest in range(rows):
                value = None
                for row in range(rows):
                    turn = (row - dest) * bins % LANES
                    moved = pltpu.roll(taken[row], turn, 1) if turn else taken[row]
                    value = moved if value is None else jnp.where(lane == row, moved, value)
                out_ref[dest, 0, part, pl.ds(m1 * depth, depth), :] = value


def pack(echo, first, count, devices):
    bins = BINS // devices
    rows = LANES // bins
    held = echo.shape[2]
    return pl.pallas_call(
        functools.partial(pack_body, rows, bins),
        grid=(count, BINS // LANES),
        in_specs=[
            pl.BlockSpec((2, rows, held, LANES), lambda u, c: (0, u + first, 0, c)),
        ],
        out_specs=pl.BlockSpec((rows, 1, 2, held, LANES), lambda u, c: (c, u, 0, 0, 0)),
        out_shape=jax.ShapeDtypeStruct((devices, count, 2, held, LANES), jnp.float32),
        cost_estimate=pl.CostEstimate(
            flops=0, bytes_accessed=16 * devices * count * held * LANES, transcendentals=0
        ),
        name="pack",
    )(echo)


def extend(ref, store):
    for m1 in range(MINOR - PAD, MINOR):
        store(m1 - MINOR + PAD, pltpu.roll(ref(m1 + PAD), 1, 0))
    for m1 in range(PAD):
        store(m1 + MINOR + PAD, pltpu.roll(ref(m1 + PAD), MAJOR - 1, 0))


def weight_body(shift_ref, fraction_ref, out_ref, taps, shifts):
    q1 = pl.program_id(0)

    @pl.when(q1 == 0)
    def _():
        coefficients = series()

        @pl.loop(0, MINOR)
        def _(m1):
            shifts[PAD + m1] = shift_ref[m1]

            @pl.loop(0, BLOCKS)
            def _(block):
                at = pl.ds(pl.multiple_of(block * 8, 8), 8)
                fraction = fraction_ref[m1, at, :]
                for tap in range(8):
                    ratio = (float(tap - 3) - fraction) / 4.0
                    inner = jnp.maximum(1.0 - ratio * ratio, 0.0)
                    total = jnp.full_like(inner, coefficients[40])
                    for order in range(39, -1, -1):
                        total = total * inner + coefficients[order]
                    taps[tap, PAD + m1, at, :] = total

        def keep(tap, row, value):
            taps[tap, row] = value

        def keep_shift(row, value):
            shifts[row] = value

        @pl.loop(0, 8)
        def _(tap):
            extend(lambda row: taps[tap, row], functools.partial(keep, tap))

        extend(lambda row: shifts[row], keep_shift)

    table, _ = windows()
    for block in range(BLOCKS):
        at = pl.ds(8 * block, 8)
        for parity in range(2):
            start, offsets = table[block][parity]
            for index, e in enumerate(offsets):
                row = q1 - e + PAD
                shift = shifts[row, at, :]
                value = jnp.zeros((8, LANES), jnp.float32)
                for tap in range(8):
                    value = jnp.where(shift == 2 * e + parity + 3 - tap, taps[tap, row, at, :], value)
                out_ref[0, start + index] = value


def weights(codes):
    _, entries = windows()
    pulse = jnp.arange(MINOR, dtype=jnp.int32)[:, None] + MINOR * jnp.arange(MAJOR, dtype=jnp.int32)[None, :]
    slow = (pulse - PULSES // 2)[:, :, None]
    numerator = 2 * slow * TONE
    denominator = TONE + codes[None, None, :]
    cell_floor = jnp.floor_divide(numerator, denominator)
    fraction = (numerator - cell_floor * denominator).astype(jnp.float32) / denominator.astype(jnp.float32)
    shift = cell_floor - 2 * slow
    whole = pl.BlockSpec((MINOR, MAJOR, LANES), lambda q: (0, 0, 0))
    spread = MINOR + 2 * PAD
    return pl.pallas_call(
        weight_body,
        grid=(MINOR,),
        in_specs=[whole, whole],
        out_specs=pl.BlockSpec((1, entries, 8, LANES), lambda q: (q, 0, 0, 0)),
        out_shape=jax.ShapeDtypeStruct((MINOR, entries, 8, LANES), jnp.float32),
        scratch_shapes=[
            pltpu.VMEM((8, spread, MAJOR, LANES), jnp.float32),
            pltpu.VMEM((spread, MAJOR, LANES), jnp.int32),
        ],
        compiler_params=pltpu.CompilerParams(vmem_limit_bytes=56 * 2**20),
        cost_estimate=pl.CostEstimate(
            flops=100 * 2**20 * 8, bytes_accessed=64 * 2**20, transcendentals=0
        ),
        name="weights",
    )(shift, fraction)


def times(value, turn, size):
    real, imag = value
    turn %= size
    if turn == 0:
        return value
    if 4 * turn == size:
        return (imag, -real)
    if 2 * turn == size:
        return (-real, -imag)
    if 4 * turn == 3 * size:
        return (-imag, real)
    if (8 * turn) % size == 0:
        half = math.sqrt(0.5)
        kind = 8 * turn // size
        if kind == 1:
            return (half * (real + imag), half * (imag - real))
        if kind == 3:
            return (half * (imag - real), -half * (real + imag))
        if kind == 5:
            return (-half * (real + imag), half * (real - imag))
        return (half * (real - imag), half * (real + imag))
    cosine = math.cos(2.0 * math.pi * turn / size)
    sine = math.sin(2.0 * math.pi * turn / size)
    return (real * cosine + imag * sine, imag * cosine - real * sine)


def plus(one, two):
    return (one[0] + two[0], one[1] + two[1])


def minus(one, two):
    return (one[0] - two[0], one[1] - two[1])


def dft4(values):
    sum_a, dif_a = plus(values[0], values[2]), minus(values[0], values[2])
    sum_b, dif_b = plus(values[1], values[3]), minus(values[1], values[3])
    side = (dif_b[1], -dif_b[0])
    return [plus(sum_a, sum_b), plus(dif_a, side), minus(sum_a, sum_b), minus(dif_a, side)]


def dft16(load):
    columns = []
    for low in range(4):
        done = dft4([load(low + 4 * high) for high in range(4)])
        columns.append([times(done[k], low * k, 16) for k in range(4)])
    result = [None] * 16
    for k in range(4):
        done = dft4([columns[low][k] for low in range(4)])
        for high in range(4):
            result[k + 4 * high] = done[high]
    return result


def main_body(first, count, rows, bins, has_base, recv_ref, weight_ref, turn_ref, scale_ref, *rest):
    if has_base:
        rest = rest[1:]
    out_ref, spread, pairs, mids, tall, wide, sem = rest
    q1 = pl.program_id(0)
    devices, depth = recv_ref.shape[0], recv_ref.shape[3] // MINOR

    @pl.when(q1 == 0)
    def _():
        for unit in range(count):
            for part in range(2):
                @pl.loop(0, MINOR)
                def _(m1):
                    for device in range(devices):
                        at = pl.ds(pl.multiple_of(m1 * depth, depth), depth)
                        spread[PAD + m1, part, unit, pl.ds(device * depth, depth), :] = recv_ref[device, unit, part, at, :]

                def keep(row, value):
                    spread[row, part, unit] = value

                extend(lambda row: spread[row, part, unit], keep)

    table, _ = windows()
    for parity in range(2):
        for block in range(BLOCKS):
            start, offsets = table[block][parity]
            sums = [[None] * count, [None] * count]
            for index, e in enumerate(offsets):
                weight = weight_ref[0, start + index]
                row = q1 - e + PAD
                for part in range(2):
                    for unit in range(count):
                        term = weight * spread[row, part, unit, pl.ds(8 * block, 8), :]
                        held = sums[part][unit]
                        sums[part][unit] = term if held is None else held + term
            for part in range(2):
                for unit in range(count):
                    pairs[parity, pl.ds(part * MAJOR + 8 * block, 8), pl.ds(unit * LANES, LANES)] = sums[part][unit]
    for parity in range(2):
        full = pairs[parity]
        high = full.astype(jnp.bfloat16)
        low = (full - high.astype(jnp.float32)).astype(jnp.bfloat16)
        turn_high, turn_low = turn_ref[0, parity, 0], turn_ref[0, parity, 1]
        dot = functools.partial(jnp.dot, preferred_element_type=jnp.float32)
        mids[q1, parity] = dot(turn_high, high) + (dot(turn_high, low) + dot(turn_low, high))

    @pl.when(q1 == MINOR - 1)
    def _():
        for unit in range(count):
            across = pl.ds(unit * LANES, LANES)

            @pl.loop(0, BLOCKS)
            def _(block):
                def load(parity, q):
                    return tuple(
                        mids[q, parity, pl.ds(pl.multiple_of(part * MAJOR + 8 * block, 8), 8), across]
                        for part in range(2)
                    )

                even = dft16(functools.partial(load, 0))
                odd = dft16(functools.partial(load, 1))
                for n1 in range(16):
                    k = n1 - 8
                    value = plus(even[k % 16], times(odd[k % 16], k, 32))
                    for part in range(2):
                        tall[part, n1, pl.ds(pl.multiple_of(8 * block, 8), 8), :] = value[part]

            @pl.loop(0, 16)
            def _(n1):
                at = pl.ds(pl.multiple_of(n1 * LANES, LANES), LANES)
                scale = scale_ref[pl.ds(0, 1), at]
                for part in range(2):
                    turned = jnp.transpose(tall[part, n1]) * scale
                    for row in range(rows):
                        wide[part, unit * rows + row, :, at] = turned[row * bins : (row + 1) * bins]

            copy = pltpu.make_async_copy(
                wide.at[:, pl.ds(unit * rows, rows)],
                out_ref.at[:, pl.ds((first + unit) * rows, rows)],
                sem.at[unit],
            )
            copy.start()
        for unit in range(count):
            pltpu.make_async_copy(
                wide.at[:, pl.ds(unit * rows, rows)],
                out_ref.at[:, pl.ds((first + unit) * rows, rows)],
                sem.at[unit],
            ).wait()


def finish(recv, weight, turn, scale, base, first, total):
    devices, count = recv.shape[0], recv.shape[1]
    bins = BINS // devices
    rows = LANES // bins
    _, entries = windows()
    one = pl.Buffered(1)
    in_specs = [
        pl.BlockSpec(recv.shape, lambda q: (0, 0, 0, 0, 0), pipeline_mode=one),
        pl.BlockSpec((1, entries, 8, LANES), lambda q: (q, 0, 0, 0)),
        pl.BlockSpec((1, 2, 2, 2 * MAJOR, 2 * MAJOR), lambda q: (q, 0, 0, 0, 0)),
        pl.BlockSpec((1, PULSES), lambda q: (0, 0)),
    ]
    args = [recv, weight, turn, scale]
    if base is not None:
        in_specs.append(pl.BlockSpec(memory_space=pl.ANY))
        args.append(base)
    return pl.pallas_call(
        functools.partial(main_body, first, count, rows, bins, base is not None),
        grid=(MINOR,),
        in_specs=in_specs,
        out_specs=pl.BlockSpec(memory_space=pl.ANY),
        out_shape=jax.ShapeDtypeStruct((2, total, bins, PULSES), jnp.float32),
        scratch_shapes=[
            pltpu.VMEM((MINOR + 2 * PAD, 2, count, MAJOR, LANES), jnp.float32),
            pltpu.VMEM((2, 2 * MAJOR, count * LANES), jnp.float32),
            pltpu.VMEM((MINOR, 2, 2 * MAJOR, count * LANES), jnp.float32),
            pltpu.VMEM((2, 16, MAJOR, LANES), jnp.float32),
            pltpu.VMEM((2, count * rows, bins, PULSES), jnp.float32),
            pltpu.SemaphoreType.DMA((count,)),
        ],
        input_output_aliases={} if base is None else {4: 0},
        compiler_params=pltpu.CompilerParams(vmem_limit_bytes=58 * 2**20),
        cost_estimate=pl.CostEstimate(
            flops=count * 32 * 6 * 256 * 256 * 128, bytes_accessed=(36 + 4 * count) * 2**20, transcendentals=0
        ),
        name="finish",
    )(*args)


def on_device(devices, echo, spectral_shift_units):
    bins = BINS // devices
    rows = LANES // bins
    lead = echo.shape[1] * echo.shape[2]
    flat = echo.reshape((2, lead) + echo.shape[3:])
    units = lead // rows
    cuts = (0, units - 1, units) if units > 1 else (0, units)
    codes = lax.dynamic_slice_in_dim(spectral_shift_units, lax.axis_index("pulse") * bins, bins, 0)
    received = []
    for first, last in zip(cuts[:-1], cuts[1:]):
        sent = pack(flat, first, last - first, devices)
        received.append(lax.all_to_all(sent, "pulse", 0, 0, tiled=True))
    weight = weights(jnp.tile(codes, rows))
    turn = jnp.asarray(turns())
    scale = correction(PULSES).reshape(1, PULSES)
    out = None
    for first, recv in zip(cuts[:-1], received):
        out = finish(recv, weight, turn, scale, out, first, lead)
    return out.reshape(echo.shape[:3] + (bins, PULSES))


def solution(mesh):
    placed = (P(None, "grp", None, "pulse", None), P())
    return jax.shard_map(
        functools.partial(on_device, mesh.shape["pulse"]),
        mesh=mesh,
        in_specs=placed,
        out_specs=P(None, "grp", None, "pulse", None),
        check_vma=False,
    )
```

```python
import functools
import math

import jax
import jax.numpy as jnp
import numpy as np
from jax import lax
from jax.experimental import pallas as pl
from jax.experimental.pallas import tpu as pltpu
from jax.sharding import PartitionSpec as P

PULSES = 2048
BINS = 1024
TONE = 16 * PULSES
CODE_MAX = PULSES // 8
MINOR = 16
MAJOR = PULSES // MINOR
PAD = 10
BLOCKS = MAJOR // 8
LANES = 128

BETA_KB = math.pi * math.sqrt(35.2)


def bessel_zero(value):
    quarter = value * value * 0.25
    term = jnp.ones_like(value)
    total = jnp.ones_like(value)
    for order in range(1, 41):
        term = term * quarter / float(order * order)
        total = total + term
    return total


def correction(number_of_echoes):
    grid_size = 2 * number_of_echoes
    doppler_bin_index = jnp.arange(number_of_echoes, dtype=jnp.int32) - number_of_echoes // 2
    phase = math.pi * 8.0 / grid_size * doppler_bin_index.astype(jnp.float32)
    root = jnp.sqrt(BETA_KB * BETA_KB - phase * phase)
    parity = (1 - 2 * (doppler_bin_index % 2)).astype(jnp.float32)
    peak = bessel_zero(BETA_KB * jnp.ones((), jnp.float32))
    return parity * peak * root / (8.0 * jnp.sinh(root)) / math.sqrt(number_of_echoes)


@functools.lru_cache(None)
def windows():
    pulse = np.arange(PULSES)
    numerator = 2 * (pulse - PULSES // 2) * TONE
    ends = np.stack([numerator // (TONE + code) - 2 * (pulse - PULSES // 2) for code in (-CODE_MAX, CODE_MAX)])
    low, high = ends.min(0) - 3, ends.max(0) + 4
    out, start = [], 0
    for block in range(BLOCKS):
        pairs = np.arange(128 * block, 128 * (block + 1))
        offsets = []
        for e in range(-PAD, PAD + 1):
            source = (pairs - e) % PULSES
            if np.any((low[source] <= 2 * e + 1) & (2 * e <= high[source])):
                offsets.append(e)
        out.append((start, tuple(offsets)))
        start += len(offsets)
    return tuple(out), start


@functools.lru_cache(None)
def series():
    terms = [1.0]
    for order in range(1, 41):
        terms.append(terms[-1] * (BETA_KB * BETA_KB / 4.0) / float(order * order))
    peak = math.fsum(terms)
    return tuple(term / peak for term in terms)


@functools.lru_cache(None)
def turns():
    r = np.arange(2 * MINOR)[:, None, None]
    n2 = np.arange(MAJOR)[None, :, None]
    q2 = np.arange(MAJOR)[None, None, :]
    angle = 2.0 * math.pi / (2 * PULSES) * ((32 * q2 + r) * n2 % (2 * PULSES))
    cosine, sine = np.cos(angle), np.sin(angle)
    full = np.concatenate(
        [np.concatenate([cosine, sine], 2), np.concatenate([-sine, cosine], 2)], 1
    )
    high = full.astype(jnp.bfloat16)
    low = (full - high.astype(np.float64)).astype(jnp.bfloat16)
    both = np.stack([high, low], 1)
    return both.reshape(MINOR, 2, 2, 2 * MAJOR, 2 * MAJOR)


def pack_body(rows, bins, echo_ref, out_ref):
    depth = echo_ref.shape[2] // MINOR
    lane = lax.broadcasted_iota(jnp.int32, (depth, LANES), 1) // bins
    for part in range(2):
        for m1 in range(MINOR):
            taken = [echo_ref[part, row, pl.ds(m1, depth, stride=MINOR), :] for row in range(rows)]
            for dest in range(rows):
                value = None
                for row in range(rows):
                    turn = (row - dest) * bins % LANES
                    moved = pltpu.roll(taken[row], turn, 1) if turn else taken[row]
                    value = moved if value is None else jnp.where(lane == row, moved, value)
                out_ref[dest, 0, part, pl.ds(m1 * depth, depth), :] = value


def pack(echo, first, count, devices):
    bins = BINS // devices
    rows = LANES // bins
    held = echo.shape[2]
    return pl.pallas_call(
        functools.partial(pack_body, rows, bins),
        grid=(count, BINS // LANES),
        in_specs=[
            pl.BlockSpec((2, rows, held, LANES), lambda u, c: (0, u + first, 0, c)),
        ],
        out_specs=pl.BlockSpec((rows, 1, 2, held, LANES), lambda u, c: (c, u, 0, 0, 0)),
        out_shape=jax.ShapeDtypeStruct((devices, count, 2, held, LANES), jnp.float32),
        cost_estimate=pl.CostEstimate(
            flops=0, bytes_accessed=16 * devices * count * held * LANES, transcendentals=0
        ),
        name="pack",
    )(echo)


def extend(ref, store):
    for m1 in range(MINOR - PAD, MINOR):
        store(m1 - MINOR + PAD, pltpu.roll(ref(m1 + PAD), 1, 0))
    for m1 in range(PAD):
        store(m1 + MINOR + PAD, pltpu.roll(ref(m1 + PAD), MAJOR - 1, 0))


def weight_body(bins, shift_ref, fraction_ref, out_ref, taps, shifts):
    q1 = pl.program_id(0)
    parity = lax.broadcasted_iota(jnp.int32, (MAJOR, LANES), 1) // bins % 2

    @pl.when(q1 == 0)
    def _():
        coefficients = series()

        @pl.loop(0, MINOR)
        def _(m1):
            shifts[PAD + m1] = shift_ref[m1] - parity

            @pl.loop(0, BLOCKS)
            def _(block):
                at = pl.ds(pl.multiple_of(block * 8, 8), 8)
                fraction = fraction_ref[m1, at, :]
                for tap in range(8):
                    ratio = (float(tap - 3) - fraction) / 4.0
                    inner = jnp.maximum(1.0 - ratio * ratio, 0.0)
                    total = jnp.full_like(inner, coefficients[40])
                    for order in range(39, -1, -1):
                        total = total * inner + coefficients[order]
                    taps[tap, PAD + m1, at, :] = total

        def keep(tap, row, value):
            taps[tap, row] = value

        def keep_shift(row, value):
            shifts[row] = value

        @pl.loop(0, 8)
        def _(tap):
            extend(lambda row: taps[tap, row], functools.partial(keep, tap))

        extend(lambda row: shifts[row], keep_shift)

    table, _ = windows()
    for block in range(BLOCKS):
        at = pl.ds(8 * block, 8)
        start, offsets = table[block]
        for index, e in enumerate(offsets):
            row = q1 - e + PAD
            shift = shifts[row, at, :]
            value = jnp.zeros((8, LANES), jnp.float32)
            for tap in range(8):
                value = jnp.where(shift == 2 * e + 3 - tap, taps[tap, row, at, :], value)
            out_ref[0, start + index] = value


def weights(codes, bins):
    _, entries = windows()
    pulse = jnp.arange(MINOR, dtype=jnp.int32)[:, None] + MINOR * jnp.arange(MAJOR, dtype=jnp.int32)[None, :]
    slow = (pulse - PULSES // 2)[:, :, None]
    numerator = 2 * slow * TONE
    denominator = TONE + codes[None, None, :]
    cell_floor = jnp.floor_divide(numerator, denominator)
    fraction = (numerator - cell_floor * denominator).astype(jnp.float32) / denominator.astype(jnp.float32)
    shift = cell_floor - 2 * slow
    whole = pl.BlockSpec((MINOR, MAJOR, LANES), lambda q: (0, 0, 0))
    spread = MINOR + 2 * PAD
    return pl.pallas_call(
        functools.partial(weight_body, bins),
        grid=(MINOR,),
        in_specs=[whole, whole],
        out_specs=pl.BlockSpec((1, entries, 8, LANES), lambda q: (q, 0, 0, 0)),
        out_shape=jax.ShapeDtypeStruct((MINOR, entries, 8, LANES), jnp.float32),
        scratch_shapes=[
            pltpu.VMEM((8, spread, MAJOR, LANES), jnp.float32),
            pltpu.VMEM((spread, MAJOR, LANES), jnp.int32),
        ],
        compiler_params=pltpu.CompilerParams(vmem_limit_bytes=56 * 2**20),
        cost_estimate=pl.CostEstimate(
            flops=100 * 2**20 * 8, bytes_accessed=64 * 2**20, transcendentals=0
        ),
        name="weights",
    )(shift, fraction)


def times(value, turn, size):
    real, imag = value
    turn %= size
    if turn == 0:
        return value
    if 4 * turn == size:
        return (imag, -real)
    if 2 * turn == size:
        return (-real, -imag)
    if 4 * turn == 3 * size:
        return (-imag, real)
    if (8 * turn) % size == 0:
        half = math.sqrt(0.5)
        kind = 8 * turn // size
        if kind == 1:
            return (half * (real + imag), half * (imag - real))
        if kind == 3:
            return (half * (imag - real), -half * (real + imag))
        if kind == 5:
            return (-half * (real + imag), half * (real - imag))
        return (half * (real - imag), half * (real + imag))
    cosine = math.cos(2.0 * math.pi * turn / size)
    sine = math.sin(2.0 * math.pi * turn / size)
    return (real * cosine + imag * sine, imag * cosine - real * sine)


def plus(one, two):
    return (one[0] + two[0], one[1] + two[1])


def minus(one, two):
    return (one[0] - two[0], one[1] - two[1])


def dft4(values):
    sum_a, dif_a = plus(values[0], values[2]), minus(values[0], values[2])
    sum_b, dif_b = plus(values[1], values[3]), minus(values[1], values[3])
    side = (dif_b[1], -dif_b[0])
    return [plus(sum_a, sum_b), plus(dif_a, side), minus(sum_a, sum_b), minus(dif_a, side)]


def dft16(load):
    columns = []
    for low in range(4):
        done = dft4([load(low + 4 * high) for high in range(4)])
        columns.append([times(done[k], low * k, 16) for k in range(4)])
    result = [None] * 16
    for k in range(4):
        done = dft4([columns[low][k] for low in range(4)])
        for high in range(4):
            result[k + 4 * high] = done[high]
    return result


def main_body(first, count, rows, bins, has_base, recv_ref, weight_ref, turn_ref, scale_ref, *rest):
    if has_base:
        rest = rest[1:]
    out_ref, spread, pairs, mids, tall, wide, sem = rest
    q1 = pl.program_id(0)
    devices, depth = recv_ref.shape[0], recv_ref.shape[3] // MINOR

    @pl.when(q1 == 0)
    def _():
        for unit in range(count):
            for part in range(2):
                @pl.loop(0, MINOR)
                def _(m1):
                    for device in range(devices):
                        at = pl.ds(pl.multiple_of(m1 * depth, depth), depth)
                        spread[PAD + m1, part, unit, pl.ds(device * depth, depth), :] = recv_ref[device, unit, part, at, :]

                def keep(row, value):
                    spread[row, part, unit] = value

                extend(lambda row: spread[row, part, unit], keep)

    table, _ = windows()
    first_parity = lax.broadcasted_iota(jnp.int32, (8, LANES), 1) // bins % 2 == 0
    for block in range(BLOCKS):
        start, offsets = table[block]
        sums = {}
        for index, e in enumerate(offsets):
            both = weight_ref[0, start + index]
            ahead = pltpu.roll(both, bins, 1)
            behind = ahead if 2 * bins == LANES else pltpu.roll(both, LANES - bins, 1)
            weight = (jnp.where(first_parity, both, ahead), jnp.where(first_parity, behind, both))
            row = q1 - e + PAD
            for part in range(2):
                for unit in range(count):
                    sample = spread[row, part, unit, pl.ds(8 * block, 8), :]
                    for parity in range(2):
                        term = weight[parity] * sample
                        key = (parity, part, unit)
                        sums[key] = sums[key] + term if key in sums else term
        for (parity, part, unit), value in sums.items():
            pairs[parity, pl.ds(part * MAJOR + 8 * block, 8), pl.ds(unit * LANES, LANES)] = value
    for parity in range(2):
        full = pairs[parity]
        high = full.astype(jnp.bfloat16)
        low = (full - high.astype(jnp.float32)).astype(jnp.bfloat16)
        turn_high, turn_low = turn_ref[0, parity, 0], turn_ref[0, parity, 1]
        dot = functools.partial(jnp.dot, preferred_element_type=jnp.float32)
        mids[q1, parity] = dot(turn_high, high) + (dot(turn_high, low) + dot(turn_low, high))

    @pl.when(q1 == MINOR - 1)
    def _():
        for unit in range(count):
            across = pl.ds(unit * LANES, LANES)

            @pl.loop(0, BLOCKS)
            def _(block):
                def load(parity, q):
                    return tuple(
                        mids[q, parity, pl.ds(pl.multiple_of(part * MAJOR + 8 * block, 8), 8), across]
                        for part in range(2)
                    )

                even = dft16(functools.partial(load, 0))
                odd = dft16(functools.partial(load, 1))
                for n1 in range(16):
                    k = n1 - 8
                    value = plus(even[k % 16], times(odd[k % 16], k, 32))
                    for part in range(2):
                        tall[part, n1, pl.ds(pl.multiple_of(8 * block, 8), 8), :] = value[part]

            @pl.loop(0, 16)
            def _(n1):
                at = pl.ds(pl.multiple_of(n1 * LANES, LANES), LANES)
                scale = scale_ref[pl.ds(0, 1), at]
                for part in range(2):
                    turned = jnp.transpose(tall[part, n1]) * scale
                    for row in range(rows):
                        wide[part, unit * rows + row, :, at] = turned[row * bins : (row + 1) * bins]

            copy = pltpu.make_async_copy(
                wide.at[:, pl.ds(unit * rows, rows)],
                out_ref.at[:, pl.ds((first + unit) * rows, rows)],
                sem.at[unit],
            )
            copy.start()
        for unit in range(count):
            pltpu.make_async_copy(
                wide.at[:, pl.ds(unit * rows, rows)],
                out_ref.at[:, pl.ds((first + unit) * rows, rows)],
                sem.at[unit],
            ).wait()


def finish(recv, weight, turn, scale, base, first, total):
    devices, count = recv.shape[0], recv.shape[1]
    bins = BINS // devices
    rows = LANES // bins
    _, entries = windows()
    one = pl.Buffered(1)
    in_specs = [
        pl.BlockSpec(recv.shape, lambda q: (0, 0, 0, 0, 0), pipeline_mode=one),
        pl.BlockSpec((1, entries, 8, LANES), lambda q: (q, 0, 0, 0)),
        pl.BlockSpec((1, 2, 2, 2 * MAJOR, 2 * MAJOR), lambda q: (q, 0, 0, 0, 0)),
        pl.BlockSpec((1, PULSES), lambda q: (0, 0)),
    ]
    args = [recv, weight, turn, scale]
    if base is not None:
        in_specs.append(pl.BlockSpec(memory_space=pl.ANY))
        args.append(base)
    return pl.pallas_call(
        functools.partial(main_body, first, count, rows, bins, base is not None),
        grid=(MINOR,),
        in_specs=in_specs,
        out_specs=pl.BlockSpec(memory_space=pl.ANY),
        out_shape=jax.ShapeDtypeStruct((2, total, bins, PULSES), jnp.float32),
        scratch_shapes=[
            pltpu.VMEM((MINOR + 2 * PAD, 2, count, MAJOR, LANES), jnp.float32),
            pltpu.VMEM((2, 2 * MAJOR, count * LANES), jnp.float32),
            pltpu.VMEM((MINOR, 2, 2 * MAJOR, count * LANES), jnp.float32),
            pltpu.VMEM((2, 16, MAJOR, LANES), jnp.float32),
            pltpu.VMEM((2, count * rows, bins, PULSES), jnp.float32),
            pltpu.SemaphoreType.DMA((count,)),
        ],
        input_output_aliases={} if base is None else {4: 0},
        compiler_params=pltpu.CompilerParams(vmem_limit_bytes=58 * 2**20),
        cost_estimate=pl.CostEstimate(
            flops=count * 32 * 6 * 256 * 256 * 128, bytes_accessed=(36 + 4 * count) * 2**20, transcendentals=0
        ),
        name="finish",
    )(*args)


def on_device(devices, echo, spectral_shift_units):
    bins = BINS // devices
    rows = LANES // bins
    lead = echo.shape[1] * echo.shape[2]
    flat = echo.reshape((2, lead) + echo.shape[3:])
    units = lead // rows
    cuts = (0, units - 1, units) if units > 1 else (0, units)
    codes = lax.dynamic_slice_in_dim(spectral_shift_units, lax.axis_index("pulse") * bins, bins, 0)
    sent = [pack(flat, first, last - first, devices) for first, last in zip(cuts[:-1], cuts[1:])]
    weight = weights(jnp.tile(codes, rows), bins)
    received = [lax.all_to_all(sent[0], "pulse", 0, 0, tiled=True)]
    for later in sent[1:]:
        later, weight = lax.optimization_barrier((later, weight))
        received.append(lax.all_to_all(later, "pulse", 0, 0, tiled=True))
    turn = jnp.asarray(turns())
    scale = correction(PULSES).reshape(1, PULSES)
    out = None
    for first, recv in zip(cuts[:-1], received):
        out = finish(recv, weight, turn, scale, out, first, lead)
    return out.reshape(echo.shape[:3] + (bins, PULSES))


def solution(mesh):
    placed = (P(None, "grp", None, "pulse", None), P())
    return jax.shard_map(
        functools.partial(on_device, mesh.shape["pulse"]),
        mesh=mesh,
        in_specs=placed,
        out_specs=P(None, "grp", None, "pulse", None),
        check_vma=False,
    )
```

```python
import functools
import math

import jax
import jax.numpy as jnp
import numpy as np
from jax import lax
from jax.experimental import pallas as pl
from jax.experimental.pallas import tpu as pltpu
from jax.sharding import PartitionSpec as P

PULSES = 2048
BINS = 1024
TONE = 16 * PULSES
CODE_MAX = PULSES // 8
MINOR = 16
MAJOR = PULSES // MINOR
PAD = 10
BLOCKS = MAJOR // 8
LANES = 128

BETA_KB = math.pi * math.sqrt(35.2)


def bessel_zero(value):
    quarter = value * value * 0.25
    term = jnp.ones_like(value)
    total = jnp.ones_like(value)
    for order in range(1, 41):
        term = term * quarter / float(order * order)
        total = total + term
    return total


def correction(number_of_echoes):
    grid_size = 2 * number_of_echoes
    doppler_bin_index = jnp.arange(number_of_echoes, dtype=jnp.int32) - number_of_echoes // 2
    phase = math.pi * 8.0 / grid_size * doppler_bin_index.astype(jnp.float32)
    root = jnp.sqrt(BETA_KB * BETA_KB - phase * phase)
    parity = (1 - 2 * (doppler_bin_index % 2)).astype(jnp.float32)
    peak = bessel_zero(BETA_KB * jnp.ones((), jnp.float32))
    return parity * peak * root / (8.0 * jnp.sinh(root)) / math.sqrt(number_of_echoes)


@functools.lru_cache(None)
def windows():
    pulse = np.arange(PULSES)
    numerator = 2 * (pulse - PULSES // 2) * TONE
    ends = np.stack([numerator // (TONE + code) - 2 * (pulse - PULSES // 2) for code in (-CODE_MAX, CODE_MAX)])
    low, high = ends.min(0) - 3, ends.max(0) + 4
    out, start = [], 0
    for block in range(BLOCKS):
        pairs = np.arange(128 * block, 128 * (block + 1))
        offsets = []
        for e in range(-PAD, PAD + 1):
            source = (pairs - e) % PULSES
            if np.any((low[source] <= 2 * e + 1) & (2 * e <= high[source])):
                offsets.append(e)
        out.append((start, tuple(offsets)))
        start += len(offsets)
    return tuple(out), start


@functools.lru_cache(None)
def series():
    terms = [1.0]
    for order in range(1, 41):
        terms.append(terms[-1] * (BETA_KB * BETA_KB / 4.0) / float(order * order))
    peak = math.fsum(terms)
    return tuple(term / peak for term in terms)


@functools.lru_cache(None)
def turns():
    r = np.arange(2 * MINOR)[:, None, None]
    n2 = np.arange(MAJOR)[None, :, None]
    q2 = np.arange(MAJOR)[None, None, :]
    angle = 2.0 * math.pi / (2 * PULSES) * ((32 * q2 + r) * n2 % (2 * PULSES))
    cosine, sine = np.cos(angle), np.sin(angle)
    full = np.concatenate(
        [np.concatenate([cosine, sine], 2), np.concatenate([-sine, cosine], 2)], 1
    )
    high = full.astype(jnp.bfloat16)
    low = (full - high.astype(np.float64)).astype(jnp.bfloat16)
    both = np.stack([high, low], 1)
    return both.reshape(MINOR, 2, 2, 2 * MAJOR, 2 * MAJOR)


def pack_body(rows, bins, echo_ref, out_ref):
    held = echo_ref.shape[2]
    depth = held // MINOR
    lane = lax.broadcasted_iota(jnp.int32, (8, LANES), 1) // bins
    for column in range(BINS // LANES):
        for group in range(held // 8):
            taken = [
                echo_ref[0, row, pl.ds(8 * group, 8), pl.ds(column * LANES, LANES)] for row in range(rows)
            ]
            to = pl.ds(8 * group % MINOR * depth + 8 * group // MINOR, 8, stride=depth)
            for dest in range(rows):
                value = None
                for row in range(rows):
                    turn = (row - dest) * bins % LANES
                    moved = pltpu.roll(taken[row], turn, 1) if turn else taken[row]
                    value = moved if value is None else jnp.where(lane == row, moved, value)
                out_ref[column * rows + dest, 0, 0, to, :] = value


def pack(echo, first, count, devices):
    bins = BINS // devices
    rows = LANES // bins
    held = echo.shape[2]
    return pl.pallas_call(
        functools.partial(pack_body, rows, bins),
        grid=(count, 2),
        in_specs=[
            pl.BlockSpec((1, rows, held, BINS), lambda u, part: (part, u + first, 0, 0)),
        ],
        out_specs=pl.BlockSpec((devices, 1, 1, held, LANES), lambda u, part: (0, u, part, 0, 0)),
        out_shape=jax.ShapeDtypeStruct((devices, count, 2, held, LANES), jnp.float32),
        compiler_params=pltpu.CompilerParams(vmem_limit_bytes=56 * 2**20),
        cost_estimate=pl.CostEstimate(
            flops=0, bytes_accessed=16 * devices * count * held * LANES, transcendentals=0
        ),
        name="pack",
    )(echo)


def extend(ref, store):
    for m1 in range(MINOR - PAD, MINOR):
        store(m1 - MINOR + PAD, pltpu.roll(ref(m1 + PAD), 1, 0))
    for m1 in range(PAD):
        store(m1 + MINOR + PAD, pltpu.roll(ref(m1 + PAD), MAJOR - 1, 0))


def weight_body(bins, shift_ref, fraction_ref, out_ref, taps, shifts):
    q1 = pl.program_id(0)
    parity = lax.broadcasted_iota(jnp.int32, (MAJOR, LANES), 1) // bins % 2

    @pl.when(q1 == 0)
    def _():
        coefficients = series()

        @pl.loop(0, MINOR)
        def _(m1):
            shifts[PAD + m1] = shift_ref[m1] - parity

            @pl.loop(0, BLOCKS)
            def _(block):
                at = pl.ds(pl.multiple_of(block * 8, 8), 8)
                fraction = fraction_ref[m1, at, :]
                for tap in range(8):
                    ratio = (float(tap - 3) - fraction) / 4.0
                    inner = jnp.maximum(1.0 - ratio * ratio, 0.0)
                    total = jnp.full_like(inner, coefficients[40])
                    for order in range(39, -1, -1):
                        total = total * inner + coefficients[order]
                    taps[tap, PAD + m1, at, :] = total

        def keep(tap, row, value):
            taps[tap, row] = value

        def keep_shift(row, value):
            shifts[row] = value

        @pl.loop(0, 8)
        def _(tap):
            extend(lambda row: taps[tap, row], functools.partial(keep, tap))

        extend(lambda row: shifts[row], keep_shift)

    table, _ = windows()
    for block in range(BLOCKS):
        at = pl.ds(8 * block, 8)
        start, offsets = table[block]
        for index, e in enumerate(offsets):
            row = q1 - e + PAD
            shift = shifts[row, at, :]
            value = jnp.zeros((8, LANES), jnp.float32)
            for tap in range(8):
                value = jnp.where(shift == 2 * e + 3 - tap, taps[tap, row, at, :], value)
            out_ref[0, start + index] = value


def weights(codes, bins):
    _, entries = windows()
    pulse = jnp.arange(MINOR, dtype=jnp.int32)[:, None] + MINOR * jnp.arange(MAJOR, dtype=jnp.int32)[None, :]
    slow = (pulse - PULSES // 2)[:, :, None]
    numerator = 2 * slow * TONE
    denominator = TONE + codes[None, None, :]
    cell_floor = jnp.floor_divide(numerator, denominator)
    fraction = (numerator - cell_floor * denominator).astype(jnp.float32) / denominator.astype(jnp.float32)
    shift = cell_floor - 2 * slow
    whole = pl.BlockSpec((MINOR, MAJOR, LANES), lambda q: (0, 0, 0))
    spread = MINOR + 2 * PAD
    return pl.pallas_call(
        functools.partial(weight_body, bins),
        grid=(MINOR,),
        in_specs=[whole, whole],
        out_specs=pl.BlockSpec((1, entries, 8, LANES), lambda q: (q, 0, 0, 0)),
        out_shape=jax.ShapeDtypeStruct((MINOR, entries, 8, LANES), jnp.float32),
        scratch_shapes=[
            pltpu.VMEM((8, spread, MAJOR, LANES), jnp.float32),
            pltpu.VMEM((spread, MAJOR, LANES), jnp.int32),
        ],
        compiler_params=pltpu.CompilerParams(vmem_limit_bytes=56 * 2**20),
        cost_estimate=pl.CostEstimate(
            flops=100 * 2**20 * 8, bytes_accessed=64 * 2**20, transcendentals=0
        ),
        name="weights",
    )(shift, fraction)


def times(value, turn, size):
    real, imag = value
    turn %= size
    if turn == 0:
        return value
    if 4 * turn == size:
        return (imag, -real)
    if 2 * turn == size:
        return (-real, -imag)
    if 4 * turn == 3 * size:
        return (-imag, real)
    if (8 * turn) % size == 0:
        half = math.sqrt(0.5)
        kind = 8 * turn // size
        if kind == 1:
            return (half * (real + imag), half * (imag - real))
        if kind == 3:
            return (half * (imag - real), -half * (real + imag))
        if kind == 5:
            return (-half * (real + imag), half * (real - imag))
        return (half * (real - imag), half * (real + imag))
    cosine = math.cos(2.0 * math.pi * turn / size)
    sine = math.sin(2.0 * math.pi * turn / size)
    return (real * cosine + imag * sine, imag * cosine - real * sine)


def plus(one, two):
    return (one[0] + two[0], one[1] + two[1])


def minus(one, two):
    return (one[0] - two[0], one[1] - two[1])


def dft4(values):
    sum_a, dif_a = plus(values[0], values[2]), minus(values[0], values[2])
    sum_b, dif_b = plus(values[1], values[3]), minus(values[1], values[3])
    side = (dif_b[1], -dif_b[0])
    return [plus(sum_a, sum_b), plus(dif_a, side), minus(sum_a, sum_b), minus(dif_a, side)]


def dft16(load):
    columns = []
    for low in range(4):
        done = dft4([load(low + 4 * high) for high in range(4)])
        columns.append([times(done[k], low * k, 16) for k in range(4)])
    result = [None] * 16
    for k in range(4):
        done = dft4([columns[low][k] for low in range(4)])
        for high in range(4):
            result[k + 4 * high] = done[high]
    return result


def main_body(first, count, rows, bins, has_base, close, recv_ref, weight_ref, turn_ref, scale_ref, *rest):
    if has_base:
        rest = rest[1:]
    out_ref, spread, pairs, mids, tall, wide, sem = rest[:7]
    q1 = pl.program_id(0)
    before = jnp.maximum(q1 - 1, 0)
    if close:
        weight_far, turn_far = weight_ref, turn_ref
        weight_ref, turn_ref, fetched = rest[7:]

        def fetch_weight(q):
            return pltpu.make_async_copy(weight_far.at[q], weight_ref.at[q], fetched.at[0, q])

        def fetch_turn(q):
            return pltpu.make_async_copy(turn_far.at[q], turn_ref.at[q], fetched.at[1, q])

        @pl.when(q1 == 0)
        def _():
            for q in range(MINOR):
                fetch_weight(q).start()
                fetch_turn(q).start()

    devices, depth = recv_ref.shape[0], recv_ref.shape[3] // MINOR

    @pl.when(q1 == 0)
    def _():
        for unit in range(count):
            for part in range(2):
                @pl.loop(0, MINOR)
                def _(m1):
                    for device in range(devices):
                        at = pl.ds(pl.multiple_of(m1 * depth, depth), depth)
                        spread[PAD + m1, part, unit, pl.ds(device * depth, depth), :] = recv_ref[device, unit, part, at, :]

                def keep(row, value):
                    spread[row, part, unit] = value

                extend(lambda row: spread[row, part, unit], keep)

    def combine():
        turn_at = before if close else 0
        dot = functools.partial(jnp.dot, preferred_element_type=jnp.float32)
        width = count * LANES
        for parity in range(2):
            full = pairs[parity]
            high = full.astype(jnp.bfloat16)
            low = (full - high.astype(jnp.float32)).astype(jnp.bfloat16)
            turn_high, turn_low = turn_ref[turn_at, parity, 0], turn_ref[turn_at, parity, 1]
            if count == 1:
                both = dot(turn_high, jnp.concatenate([high, low], 1))
                mids[before, parity] = both[:, :width] + (both[:, width:] + dot(turn_low, high))
            else:
                mids[before, parity] = dot(turn_high, high) + (dot(turn_high, low) + dot(turn_low, high))

    if close:
        @pl.when(q1 < MINOR)
        def _():
            fetch_weight(q1).wait()

        @pl.when(q1 != 1)
        def _():
            fetch_turn(before).wait()

    @pl.when(q1 < MINOR)
    def _():
        combine()
        weight_at = q1 if close else 0
        table, _ = windows()
        first_parity = lax.broadcasted_iota(jnp.int32, (8, LANES), 1) // bins % 2 == 0
        for block in range(BLOCKS):
            start, offsets = table[block]
            sums = {}
            for index, e in enumerate(offsets):
                both = weight_ref[weight_at, start + index]
                ahead = pltpu.roll(both, bins, 1)
                behind = ahead if 2 * bins == LANES else pltpu.roll(both, LANES - bins, 1)
                weight = (jnp.where(first_parity, both, ahead), jnp.where(first_parity, behind, both))
                row = q1 - e + PAD
                for part in range(2):
                    for unit in range(count):
                        sample = spread[row, part, unit, pl.ds(8 * block, 8), :]
                        for parity in range(2):
                            term = weight[parity] * sample
                            key = (parity, part, unit)
                            sums[key] = sums[key] + term if key in sums else term
            for (parity, part, unit), value in sums.items():
                pairs[parity, pl.ds(part * MAJOR + 8 * block, 8), pl.ds(unit * LANES, LANES)] = value

    def leave(unit, part):
        return pltpu.make_async_copy(
            wide.at[part],
            out_ref.at[part, pl.ds((first + unit) * rows, rows)],
            sem.at[unit, part],
        )

    @pl.when(q1 == MINOR)
    def _():
        combine()
        for unit in range(count):
            across = pl.ds(unit * LANES, LANES)

            @pl.loop(0, BLOCKS)
            def _(block):
                def load(parity, q):
                    return tuple(
                        mids[q, parity, pl.ds(pl.multiple_of(part * MAJOR + 8 * block, 8), 8), across]
                        for part in range(2)
                    )

                even = dft16(functools.partial(load, 0))
                odd = dft16(functools.partial(load, 1))
                for n1 in range(16):
                    k = n1 - 8
                    value = plus(even[k % 16], times(odd[k % 16], k, 32))
                    for part in range(2):
                        tall[part, n1, pl.ds(pl.multiple_of(8 * block, 8), 8), :] = value[part]

            for part in range(2):
                if unit:
                    leave(unit - 1, part).wait()

                @pl.loop(0, 4)
                def _(group):
                    for member in range(4):
                        n1 = 4 * group + member
                        at = pl.ds(pl.multiple_of(n1 * LANES, LANES), LANES)
                        turned = jnp.transpose(tall[part, n1]) * scale_ref[pl.ds(0, 1), at]
                        for row in range(rows):
                            wide[part, row, :, at] = turned[row * bins : (row + 1) * bins]

                leave(unit, part).start()
        for part in range(2):
            leave(count - 1, part).wait()


def finish(recv, weight, turn, scale, base, first, total):
    devices, count = recv.shape[0], recv.shape[1]
    bins = BINS // devices
    rows = LANES // bins
    _, entries = windows()
    close = count == 1
    if close:
        in_specs = [
            pl.BlockSpec(memory_space=pltpu.VMEM),
            pl.BlockSpec(memory_space=pl.ANY),
            pl.BlockSpec(memory_space=pl.ANY),
        ]
    else:
        in_specs = [
            pl.BlockSpec(recv.shape, lambda q: (0, 0, 0, 0, 0), pipeline_mode=pl.Buffered(1)),
            pl.BlockSpec((1, entries, 8, LANES), lambda q: (jnp.minimum(q, MINOR - 1), 0, 0, 0)),
            pl.BlockSpec((1, 2, 2, 2 * MAJOR, 2 * MAJOR), lambda q: (jnp.maximum(q - 1, 0), 0, 0, 0, 0)),
        ]
    in_specs.append(pl.BlockSpec((1, PULSES), lambda q: (0, 0)))
    args = [recv, weight, turn, scale]
    if base is not None:
        in_specs.append(pl.BlockSpec(memory_space=pl.ANY))
        args.append(base)
    ahead = []
    if close:
        ahead = [
            pltpu.VMEM(weight.shape, jnp.float32),
            pltpu.VMEM(turn.shape, jnp.bfloat16),
            pltpu.SemaphoreType.DMA((2, MINOR)),
        ]
    return pl.pallas_call(
        functools.partial(main_body, first, count, rows, bins, base is not None, close),
        grid=(MINOR + 1,),
        in_specs=in_specs,
        out_specs=pl.BlockSpec(memory_space=pl.ANY),
        out_shape=jax.ShapeDtypeStruct((2, total, bins, PULSES), jnp.float32),
        scratch_shapes=[
            pltpu.VMEM((MINOR + 2 * PAD, 2, count, MAJOR, LANES), jnp.float32),
            pltpu.VMEM((2, 2 * MAJOR, count * LANES), jnp.float32),
            pltpu.VMEM((MINOR, 2, 2 * MAJOR, count * LANES), jnp.float32),
            pltpu.VMEM((2, 16, MAJOR, LANES), jnp.float32),
            pltpu.VMEM((2, rows, bins, PULSES), jnp.float32),
            pltpu.SemaphoreType.DMA((count, 2)),
        ]
        + ahead,
        input_output_aliases={} if base is None else {4: 0},
        compiler_params=pltpu.CompilerParams(vmem_limit_bytes=(54 if close else 58) * 2**20),
        cost_estimate=pl.CostEstimate(
            flops=count * 32 * 6 * 256 * 256 * 128, bytes_accessed=(36 + 4 * count) * 2**20, transcendentals=0
        ),
        name="finish",
    )(*args)


def on_device(devices, echo, spectral_shift_units):
    bins = BINS // devices
    rows = LANES // bins
    lead = echo.shape[1] * echo.shape[2]
    flat = echo.reshape((2, lead) + echo.shape[3:])
    units = lead // rows
    cuts = (0, units - 1, units) if units > 1 else (0, units)
    codes = lax.dynamic_slice_in_dim(spectral_shift_units, lax.axis_index("pulse") * bins, bins, 0)
    sent = [pack(flat, first, last - first, devices) for first, last in zip(cuts[:-1], cuts[1:])]
    weight = weights(jnp.tile(codes, rows), bins)
    received = [lax.all_to_all(sent[0], "pulse", 0, 0, tiled=True)]
    for later in sent[1:]:
        later, weight = lax.optimization_barrier((later, weight))
        received.append(lax.all_to_all(later, "pulse", 0, 0, tiled=True))
    turn = jnp.asarray(turns())
    scale = correction(PULSES).reshape(1, PULSES)
    out = None
    for first, recv in zip(cuts[:-1], received):
        out = finish(recv, weight, turn, scale, out, first, lead)
    return out.reshape(echo.shape[:3] + (bins, PULSES))


def solution(mesh):
    placed = (P(None, "grp", None, "pulse", None), P())
    return jax.shard_map(
        functools.partial(on_device, mesh.shape["pulse"]),
        mesh=mesh,
        in_specs=placed,
        out_specs=P(None, "grp", None, "pulse", None),
        check_vma=False,
    )
```

```python
import functools
import math

import jax
import jax.numpy as jnp
import numpy as np
from jax import lax
from jax.experimental import pallas as pl
from jax.experimental.pallas import tpu as pltpu
from jax.sharding import PartitionSpec as P

PULSES = 2048
BINS = 1024
TONE = 16 * PULSES
CODE_MAX = PULSES // 8
MINOR = 16
MAJOR = PULSES // MINOR
PAD = 10
BLOCKS = MAJOR // 8
LANES = 128

BETA_KB = math.pi * math.sqrt(35.2)


def bessel_zero(value):
    quarter = value * value * 0.25
    term = jnp.ones_like(value)
    total = jnp.ones_like(value)
    for order in range(1, 41):
        term = term * quarter / float(order * order)
        total = total + term
    return total


def correction(number_of_echoes):
    grid_size = 2 * number_of_echoes
    doppler_bin_index = jnp.arange(number_of_echoes, dtype=jnp.int32) - number_of_echoes // 2
    phase = math.pi * 8.0 / grid_size * doppler_bin_index.astype(jnp.float32)
    root = jnp.sqrt(BETA_KB * BETA_KB - phase * phase)
    parity = (1 - 2 * (doppler_bin_index % 2)).astype(jnp.float32)
    peak = bessel_zero(BETA_KB * jnp.ones((), jnp.float32))
    return parity * peak * root / (8.0 * jnp.sinh(root)) / math.sqrt(number_of_echoes)


@functools.lru_cache(None)
def windows():
    pulse = np.arange(PULSES)
    numerator = 2 * (pulse - PULSES // 2) * TONE
    ends = np.stack([numerator // (TONE + code) - 2 * (pulse - PULSES // 2) for code in (-CODE_MAX, CODE_MAX)])
    low, high = ends.min(0) - 3, ends.max(0) + 4
    out, start = [], 0
    for block in range(BLOCKS):
        pairs = np.arange(128 * block, 128 * (block + 1))
        offsets = []
        for e in range(-PAD, PAD + 1):
            source = (pairs - e) % PULSES
            if np.any((low[source] <= 2 * e + 1) & (2 * e <= high[source])):
                offsets.append(e)
        out.append((start, tuple(offsets)))
        start += len(offsets)
    return tuple(out), start


@functools.lru_cache(None)
def series():
    terms = [1.0]
    for order in range(1, 41):
        terms.append(terms[-1] * (BETA_KB * BETA_KB / 4.0) / float(order * order))
    peak = math.fsum(terms)
    return tuple(term / peak for term in terms)


@functools.lru_cache(None)
def turns():
    r = np.arange(2 * MINOR)[:, None, None]
    n2 = np.arange(MAJOR)[None, :, None]
    q2 = np.arange(MAJOR)[None, None, :]
    angle = 2.0 * math.pi / (2 * PULSES) * ((32 * q2 + r) * n2 % (2 * PULSES))
    cosine, sine = np.cos(angle), np.sin(angle)
    full = np.concatenate(
        [np.concatenate([cosine, sine], 2), np.concatenate([-sine, cosine], 2)], 1
    )
    high = full.astype(jnp.bfloat16)
    low = (full - high.astype(np.float64)).astype(jnp.bfloat16)
    both = np.stack([high, low], 1)
    return both.reshape(MINOR, 2, 2, 2 * MAJOR, 2 * MAJOR)


def pack_body(rows, bins, first, pieces, echo_ref, out_ref, taken, ready, taking, leaving):
    held = echo_ref.shape[2]
    depth = held // MINOR
    lane = lax.broadcasted_iota(jnp.int32, (8, LANES), 1) // bins

    def take(piece):
        source = echo_ref.at[piece % 2, pl.ds((first + piece // 2) * rows, rows)]
        return pltpu.make_async_copy(source, taken.at[piece], taking.at[piece])

    def leave(piece):
        return pltpu.make_async_copy(ready.at[piece], out_ref.at[:, piece // 2, piece % 2], leaving.at[piece])

    for piece in range(pieces):
        take(piece).start()

    @pl.loop(0, pieces)
    def _(piece):
        take(piece).wait()
        for column in range(BINS // LANES):
            for group in range(held // 8):
                values = [
                    taken[piece, row, pl.ds(8 * group, 8), pl.ds(column * LANES, LANES)] for row in range(rows)
                ]
                to = pl.ds(8 * group % MINOR * depth + 8 * group // MINOR, 8, stride=depth)
                for dest in range(rows):
                    value = None
                    for row in range(rows):
                        turn = (row - dest) * bins % LANES
                        moved = pltpu.roll(values[row], turn, 1) if turn else values[row]
                        value = moved if value is None else jnp.where(lane == row, moved, value)
                    ready[piece, column * rows + dest, to, :] = value
        leave(piece).start()

    @pl.loop(0, pieces)
    def _(piece):
        leave(piece).wait()


def pack(echo, first, count, devices):
    bins = BINS // devices
    rows = LANES // bins
    held = echo.shape[2]
    pieces = 2 * count
    return pl.pallas_call(
        functools.partial(pack_body, rows, bins, first, pieces),
        in_specs=[pl.BlockSpec(memory_space=pl.ANY)],
        out_specs=pl.BlockSpec(memory_space=pl.ANY),
        out_shape=jax.ShapeDtypeStruct((devices, count, 2, held, LANES), jnp.float32),
        scratch_shapes=[
            pltpu.VMEM((pieces, rows, held, BINS), jnp.float32),
            pltpu.VMEM((pieces, devices, held, LANES), jnp.float32),
            pltpu.SemaphoreType.DMA((pieces,)),
            pltpu.SemaphoreType.DMA((pieces,)),
        ],
        compiler_params=pltpu.CompilerParams(vmem_limit_bytes=56 * 2**20),
        cost_estimate=pl.CostEstimate(
            flops=0, bytes_accessed=16 * devices * count * held * LANES, transcendentals=0
        ),
        name="pack",
    )(echo)


def extend(ref, store):
    for m1 in range(MINOR - PAD, MINOR):
        store(m1 - MINOR + PAD, pltpu.roll(ref(m1 + PAD), 1, 0))
    for m1 in range(PAD):
        store(m1 + MINOR + PAD, pltpu.roll(ref(m1 + PAD), MAJOR - 1, 0))


def weight_body(bins, shift_ref, fraction_ref, out_ref, taps, shifts):
    q1 = pl.program_id(0)
    parity = lax.broadcasted_iota(jnp.int32, (MAJOR, LANES), 1) // bins % 2

    @pl.when(q1 == 0)
    def _():
        coefficients = series()

        @pl.loop(0, MINOR)
        def _(m1):
            shifts[PAD + m1] = shift_ref[m1] - parity

            @pl.loop(0, BLOCKS)
            def _(block):
                at = pl.ds(pl.multiple_of(block * 8, 8), 8)
                fraction = fraction_ref[m1, at, :]
                for tap in range(8):
                    ratio = (float(tap - 3) - fraction) / 4.0
                    inner = jnp.maximum(1.0 - ratio * ratio, 0.0)
                    total = jnp.full_like(inner, coefficients[40])
                    for order in range(39, -1, -1):
                        total = total * inner + coefficients[order]
                    taps[tap, PAD + m1, at, :] = total

        def keep(tap, row, value):
            taps[tap, row] = value

        def keep_shift(row, value):
            shifts[row] = value

        @pl.loop(0, 8)
        def _(tap):
            extend(lambda row: taps[tap, row], functools.partial(keep, tap))

        extend(lambda row: shifts[row], keep_shift)

    table, _ = windows()
    for block in range(BLOCKS):
        at = pl.ds(8 * block, 8)
        start, offsets = table[block]
        for index, e in enumerate(offsets):
            row = q1 - e + PAD
            shift = shifts[row, at, :]
            value = jnp.zeros((8, LANES), jnp.float32)
            for tap in range(8):
                value = jnp.where(shift == 2 * e + 3 - tap, taps[tap, row, at, :], value)
            out_ref[0, start + index] = value


def weights(codes, bins):
    _, entries = windows()
    pulse = jnp.arange(MINOR, dtype=jnp.int32)[:, None] + MINOR * jnp.arange(MAJOR, dtype=jnp.int32)[None, :]
    slow = (pulse - PULSES // 2)[:, :, None]
    numerator = 2 * slow * TONE
    denominator = TONE + codes[None, None, :]
    cell_floor = jnp.floor_divide(numerator, denominator)
    fraction = (numerator - cell_floor * denominator).astype(jnp.float32) / denominator.astype(jnp.float32)
    shift = cell_floor - 2 * slow
    whole = pl.BlockSpec((MINOR, MAJOR, LANES), lambda q: (0, 0, 0))
    spread = MINOR + 2 * PAD
    return pl.pallas_call(
        functools.partial(weight_body, bins),
        grid=(MINOR,),
        in_specs=[whole, whole],
        out_specs=pl.BlockSpec((1, entries, 8, LANES), lambda q: (q, 0, 0, 0)),
        out_shape=jax.ShapeDtypeStruct((MINOR, entries, 8, LANES), jnp.float32),
        scratch_shapes=[
            pltpu.VMEM((8, spread, MAJOR, LANES), jnp.float32),
            pltpu.VMEM((spread, MAJOR, LANES), jnp.int32),
        ],
        compiler_params=pltpu.CompilerParams(vmem_limit_bytes=56 * 2**20),
        cost_estimate=pl.CostEstimate(
            flops=100 * 2**20 * 8, bytes_accessed=64 * 2**20, transcendentals=0
        ),
        name="weights",
    )(shift, fraction)


def times(value, turn, size):
    real, imag = value
    turn %= size
    if turn == 0:
        return value
    if 4 * turn == size:
        return (imag, -real)
    if 2 * turn == size:
        return (-real, -imag)
    if 4 * turn == 3 * size:
        return (-imag, real)
    if (8 * turn) % size == 0:
        half = math.sqrt(0.5)
        kind = 8 * turn // size
        if kind == 1:
            return (half * (real + imag), half * (imag - real))
        if kind == 3:
            return (half * (imag - real), -half * (real + imag))
        if kind == 5:
            return (-half * (real + imag), half * (real - imag))
        return (half * (real - imag), half * (real + imag))
    cosine = math.cos(2.0 * math.pi * turn / size)
    sine = math.sin(2.0 * math.pi * turn / size)
    return (real * cosine + imag * sine, imag * cosine - real * sine)


def plus(one, two):
    return (one[0] + two[0], one[1] + two[1])


def minus(one, two):
    return (one[0] - two[0], one[1] - two[1])


def dft4(values):
    sum_a, dif_a = plus(values[0], values[2]), minus(values[0], values[2])
    sum_b, dif_b = plus(values[1], values[3]), minus(values[1], values[3])
    side = (dif_b[1], -dif_b[0])
    return [plus(sum_a, sum_b), plus(dif_a, side), minus(sum_a, sum_b), minus(dif_a, side)]


def dft16(load):
    columns = []
    for low in range(4):
        done = dft4([load(low + 4 * high) for high in range(4)])
        columns.append([times(done[k], low * k, 16) for k in range(4)])
    result = [None] * 16
    for k in range(4):
        done = dft4([columns[low][k] for low in range(4)])
        for high in range(4):
            result[k + 4 * high] = done[high]
    return result


def main_body(first, count, rows, bins, has_base, close, recv_ref, weight_ref, turn_ref, scale_ref, *rest):
    if has_base:
        rest = rest[1:]
    out_ref, spread, pairs, mids, tall, wide, sem = rest[:7]
    q1 = pl.program_id(0)
    before = jnp.maximum(q1 - 1, 0)
    if close:
        weight_far, turn_far = weight_ref, turn_ref
        weight_ref, turn_ref, fetched = rest[7:]

        def fetch_weight(q):
            return pltpu.make_async_copy(weight_far.at[q], weight_ref.at[q], fetched.at[0, q])

        def fetch_turn(q):
            return pltpu.make_async_copy(turn_far.at[q], turn_ref.at[q], fetched.at[1, q])

        @pl.when(q1 == 0)
        def _():
            for q in range(MINOR):
                fetch_weight(q).start()
                fetch_turn(q).start()

    devices, depth = recv_ref.shape[0], recv_ref.shape[3] // MINOR

    @pl.when(q1 == 0)
    def _():
        for unit in range(count):
            for part in range(2):
                @pl.loop(0, MINOR)
                def _(m1):
                    for device in range(devices):
                        at = pl.ds(pl.multiple_of(m1 * depth, depth), depth)
                        spread[PAD + m1, part, unit, pl.ds(device * depth, depth), :] = recv_ref[device, unit, part, at, :]

                def keep(row, value):
                    spread[row, part, unit] = value

                extend(lambda row: spread[row, part, unit], keep)

    def combine():
        turn_at = before if close else 0
        dot = functools.partial(jnp.dot, preferred_element_type=jnp.float32)
        width = count * LANES
        for parity in range(2):
            full = pairs[parity]
            high = full.astype(jnp.bfloat16)
            low = (full - high.astype(jnp.float32)).astype(jnp.bfloat16)
            turn_high, turn_low = turn_ref[turn_at, parity, 0], turn_ref[turn_at, parity, 1]
            if count == 1:
                both = dot(turn_high, jnp.concatenate([high, low], 1))
                mids[before, parity] = both[:, :width] + (both[:, width:] + dot(turn_low, high))
            else:
                mids[before, parity] = dot(turn_high, high) + (dot(turn_high, low) + dot(turn_low, high))

    if close:
        @pl.when(q1 < MINOR)
        def _():
            fetch_weight(q1).wait()

        @pl.when(q1 != 1)
        def _():
            fetch_turn(before).wait()

    @pl.when(q1 < MINOR)
    def _():
        combine()
        weight_at = q1 if close else 0
        table, _ = windows()
        first_parity = lax.broadcasted_iota(jnp.int32, (8, LANES), 1) // bins % 2 == 0
        for block in range(BLOCKS):
            start, offsets = table[block]
            sums = {}
            for index, e in enumerate(offsets):
                weight = weight_ref[weight_at, start + index]
                weight = (weight, pltpu.roll(weight, bins, 1))
                row = q1 - e + PAD
                for part in range(2):
                    for unit in range(count):
                        sample = spread[row, part, unit, pl.ds(8 * block, 8), :]
                        for turn in range(2):
                            term = weight[turn] * sample
                            key = (turn, part, unit)
                            sums[key] = sums[key] + term if key in sums else term
            for part in range(2):
                for unit in range(count):
                    own, other = sums[0, part, unit], sums[1, part, unit]
                    at = (pl.ds(part * MAJOR + 8 * block, 8), pl.ds(unit * LANES, LANES))
                    pairs[(0,) + at] = jnp.where(first_parity, own, other)
                    pairs[(1,) + at] = jnp.where(first_parity, other, own)

    def leave(unit, part):
        return pltpu.make_async_copy(
            wide.at[part],
            out_ref.at[part, pl.ds((first + unit) * rows, rows)],
            sem.at[unit, part],
        )

    @pl.when(q1 == MINOR)
    def _():
        combine()
        for unit in range(count):
            across = pl.ds(unit * LANES, LANES)

            @pl.loop(0, BLOCKS)
            def _(block):
                def load(parity, q):
                    return tuple(
                        mids[q, parity, pl.ds(pl.multiple_of(part * MAJOR + 8 * block, 8), 8), across]
                        for part in range(2)
                    )

                even = dft16(functools.partial(load, 0))
                odd = dft16(functools.partial(load, 1))
                for n1 in range(16):
                    k = n1 - 8
                    value = plus(even[k % 16], times(odd[k % 16], k, 32))
                    for part in range(2):
                        tall[part, n1, pl.ds(pl.multiple_of(8 * block, 8), 8), :] = value[part]

            for part in range(2):
                if unit:
                    leave(unit - 1, part).wait()

                @pl.loop(0, 4)
                def _(group):
                    for member in range(4):
                        n1 = 4 * group + member
                        at = pl.ds(pl.multiple_of(n1 * LANES, LANES), LANES)
                        turned = jnp.transpose(tall[part, n1]) * scale_ref[pl.ds(0, 1), at]
                        for row in range(rows):
                            wide[part, row, :, at] = turned[row * bins : (row + 1) * bins]

                leave(unit, part).start()
        for part in range(2):
            leave(count - 1, part).wait()


def finish(recv, weight, turn, scale, base, first, total):
    devices, count = recv.shape[0], recv.shape[1]
    bins = BINS // devices
    rows = LANES // bins
    _, entries = windows()
    close = count == 1
    if close:
        in_specs = [
            pl.BlockSpec(memory_space=pltpu.VMEM),
            pl.BlockSpec(memory_space=pl.ANY),
            pl.BlockSpec(memory_space=pl.ANY),
        ]
    else:
        in_specs = [
            pl.BlockSpec(recv.shape, lambda q: (0, 0, 0, 0, 0), pipeline_mode=pl.Buffered(1)),
            pl.BlockSpec((1, entries, 8, LANES), lambda q: (jnp.minimum(q, MINOR - 1), 0, 0, 0)),
            pl.BlockSpec((1, 2, 2, 2 * MAJOR, 2 * MAJOR), lambda q: (jnp.maximum(q - 1, 0), 0, 0, 0, 0)),
        ]
    in_specs.append(pl.BlockSpec((1, PULSES), lambda q: (0, 0)))
    args = [recv, weight, turn, scale]
    if base is not None:
        in_specs.append(pl.BlockSpec(memory_space=pl.ANY))
        args.append(base)
    ahead = []
    if close:
        ahead = [
            pltpu.VMEM(weight.shape, jnp.float32),
            pltpu.VMEM(turn.shape, jnp.bfloat16),
            pltpu.SemaphoreType.DMA((2, MINOR)),
        ]
    return pl.pallas_call(
        functools.partial(main_body, first, count, rows, bins, base is not None, close),
        grid=(MINOR + 1,),
        in_specs=in_specs,
        out_specs=pl.BlockSpec(memory_space=pl.ANY),
        out_shape=jax.ShapeDtypeStruct((2, total, bins, PULSES), jnp.float32),
        scratch_shapes=[
            pltpu.VMEM((MINOR + 2 * PAD, 2, count, MAJOR, LANES), jnp.float32),
            pltpu.VMEM((2, 2 * MAJOR, count * LANES), jnp.float32),
            pltpu.VMEM((MINOR, 2, 2 * MAJOR, count * LANES), jnp.float32),
            pltpu.VMEM((2, 16, MAJOR, LANES), jnp.float32),
            pltpu.VMEM((2, rows, bins, PULSES), jnp.float32),
            pltpu.SemaphoreType.DMA((count, 2)),
        ]
        + ahead,
        input_output_aliases={} if base is None else {4: 0},
        compiler_params=pltpu.CompilerParams(vmem_limit_bytes=(48 if close else 58) * 2**20),
        cost_estimate=pl.CostEstimate(
            flops=count * 32 * 6 * 256 * 256 * 128, bytes_accessed=(36 + 4 * count) * 2**20, transcendentals=0
        ),
        name="finish",
    )(*args)


def on_device(devices, echo, spectral_shift_units):
    bins = BINS // devices
    rows = LANES // bins
    lead = echo.shape[1] * echo.shape[2]
    flat = echo.reshape((2, lead) + echo.shape[3:])
    units = lead // rows
    cuts = (0, units - 1, units) if units > 1 else (0, units)
    codes = lax.dynamic_slice_in_dim(spectral_shift_units, lax.axis_index("pulse") * bins, bins, 0)
    sent = [pack(flat, first, last - first, devices) for first, last in zip(cuts[:-1], cuts[1:])]
    weight = weights(jnp.tile(codes, rows), bins)
    received = [lax.all_to_all(sent[0], "pulse", 0, 0, tiled=True)]
    for later in sent[1:]:
        later, weight = lax.optimization_barrier((later, weight))
        received.append(lax.all_to_all(later, "pulse", 0, 0, tiled=True))
    turn = jnp.asarray(turns())
    scale = correction(PULSES).reshape(1, PULSES)
    out = None
    for first, recv in zip(cuts[:-1], received):
        out = finish(recv, weight, turn, scale, out, first, lead)
    return out.reshape(echo.shape[:3] + (bins, PULSES))


def solution(mesh):
    placed = (P(None, "grp", None, "pulse", None), P())
    return jax.shard_map(
        functools.partial(on_device, mesh.shape["pulse"]),
        mesh=mesh,
        in_specs=placed,
        out_specs=P(None, "grp", None, "pulse", None),
        check_vma=False,
    )
```

```python
import functools
import math

import jax
import jax.numpy as jnp
import numpy as np
from jax import lax
from jax.experimental import pallas as pl
from jax.experimental.pallas import tpu as pltpu
from jax.sharding import PartitionSpec as P

PULSES = 2048
BINS = 1024
TONE = 16 * PULSES
CODE_MAX = PULSES // 8
MINOR = 16
MAJOR = PULSES // MINOR
PAD = 10
BLOCKS = MAJOR // 8
LANES = 128
AHEAD = 6
CUTS = 2

BETA_KB = math.pi * math.sqrt(35.2)


def bessel_zero(value):
    quarter = value * value * 0.25
    term = jnp.ones_like(value)
    total = jnp.ones_like(value)
    for order in range(1, 41):
        term = term * quarter / float(order * order)
        total = total + term
    return total


def correction(number_of_echoes):
    grid_size = 2 * number_of_echoes
    doppler_bin_index = jnp.arange(number_of_echoes, dtype=jnp.int32) - number_of_echoes // 2
    phase = math.pi * 8.0 / grid_size * doppler_bin_index.astype(jnp.float32)
    root = jnp.sqrt(BETA_KB * BETA_KB - phase * phase)
    parity = (1 - 2 * (doppler_bin_index % 2)).astype(jnp.float32)
    peak = bessel_zero(BETA_KB * jnp.ones((), jnp.float32))
    return parity * peak * root / (8.0 * jnp.sinh(root)) / math.sqrt(number_of_echoes)


@functools.lru_cache(None)
def windows():
    pulse = np.arange(PULSES)
    numerator = 2 * (pulse - PULSES // 2) * TONE
    ends = np.stack([numerator // (TONE + code) - 2 * (pulse - PULSES // 2) for code in (-CODE_MAX, CODE_MAX)])
    low, high = ends.min(0) - 3, ends.max(0) + 4
    out, start = [], 0
    for block in range(BLOCKS):
        pairs = np.arange(128 * block, 128 * (block + 1))
        offsets = []
        for e in range(-PAD, PAD + 1):
            source = (pairs - e) % PULSES
            if np.any((low[source] <= 2 * e + 1) & (2 * e <= high[source])):
                offsets.append(e)
        out.append((start, tuple(offsets)))
        start += len(offsets)
    return tuple(out), start


@functools.lru_cache(None)
def series():
    terms = [1.0]
    for order in range(1, 41):
        terms.append(terms[-1] * (BETA_KB * BETA_KB / 4.0) / float(order * order))
    peak = math.fsum(terms)
    return tuple(term / peak for term in terms)


@functools.lru_cache(None)
def turns():
    r = np.arange(2 * MINOR)[:, None, None]
    n2 = np.arange(MAJOR)[None, :, None]
    q2 = np.arange(MAJOR)[None, None, :]
    angle = 2.0 * math.pi / (2 * PULSES) * ((32 * q2 + r) * n2 % (2 * PULSES))
    cosine, sine = np.cos(angle), np.sin(angle)
    full = np.concatenate(
        [np.concatenate([cosine, sine], 2), np.concatenate([-sine, cosine], 2)], 1
    )
    high = full.astype(jnp.bfloat16)
    low = (full - high.astype(np.float64)).astype(jnp.bfloat16)
    both = np.stack([high, low], 1)
    return both.reshape(MINOR, 2, 2, 2 * MAJOR, 2 * MAJOR)


def pack_body(rows, bins, first, pieces, echo_ref, out_ref, taken, ready, taking, leaving):
    held = echo_ref.shape[2]
    depth = held // MINOR
    lane = lax.broadcasted_iota(jnp.int32, (8, LANES), 1) // bins

    def take(piece):
        source = echo_ref.at[piece % 2, pl.ds((first + piece // 2) * rows, rows)]
        return pltpu.make_async_copy(source, taken.at[piece], taking.at[piece])

    def leave(piece):
        return pltpu.make_async_copy(ready.at[piece], out_ref.at[:, piece // 2, piece % 2], leaving.at[piece])

    for piece in range(min(AHEAD, pieces)):
        take(piece).start()

    @pl.loop(0, pieces)
    def _(piece):
        take(piece).wait()

        @pl.when(piece + AHEAD < pieces)
        def _():
            take(piece + AHEAD).start()

        for column in range(BINS // LANES):
            for group in range(held // 8):
                values = [
                    taken[piece, row, pl.ds(8 * group, 8), pl.ds(column * LANES, LANES)] for row in range(rows)
                ]
                to = pl.ds(8 * group % MINOR * depth + 8 * group // MINOR, 8, stride=depth)
                for dest in range(rows):
                    value = None
                    for row in range(rows):
                        turn = (row - dest) * bins % LANES
                        moved = pltpu.roll(values[row], turn, 1) if turn else values[row]
                        value = moved if value is None else jnp.where(lane == row, moved, value)
                    ready[piece, column * rows + dest, to, :] = value
        leave(piece).start()

    @pl.loop(0, pieces)
    def _(piece):
        leave(piece).wait()


def pack(echo, first, count, devices):
    bins = BINS // devices
    rows = LANES // bins
    held = echo.shape[2]
    pieces = 2 * count
    return pl.pallas_call(
        functools.partial(pack_body, rows, bins, first, pieces),
        in_specs=[pl.BlockSpec(memory_space=pl.ANY)],
        out_specs=pl.BlockSpec(memory_space=pl.ANY),
        out_shape=jax.ShapeDtypeStruct((devices, count, 2, held, LANES), jnp.float32),
        scratch_shapes=[
            pltpu.VMEM((pieces, rows, held, BINS), jnp.float32),
            pltpu.VMEM((pieces, devices, held, LANES), jnp.float32),
            pltpu.SemaphoreType.DMA((pieces,)),
            pltpu.SemaphoreType.DMA((pieces,)),
        ],
        compiler_params=pltpu.CompilerParams(vmem_limit_bytes=56 * 2**20),
        cost_estimate=pl.CostEstimate(
            flops=0, bytes_accessed=16 * devices * count * held * LANES, transcendentals=0
        ),
        name="pack",
    )(echo)


def extend(ref, store):
    for m1 in range(MINOR - PAD, MINOR):
        store(m1 - MINOR + PAD, pltpu.roll(ref(m1 + PAD), 1, 0))
    for m1 in range(PAD):
        store(m1 + MINOR + PAD, pltpu.roll(ref(m1 + PAD), MAJOR - 1, 0))


def weight_body(bins, shift_ref, fraction_ref, out_ref, taps, shifts):
    q1 = pl.program_id(0)
    parity = lax.broadcasted_iota(jnp.int32, (MAJOR, LANES), 1) // bins % 2

    @pl.when(q1 == 0)
    def _():
        coefficients = series()

        @pl.loop(0, MINOR)
        def _(m1):
            shifts[PAD + m1] = shift_ref[m1] - parity

            @pl.loop(0, BLOCKS)
            def _(block):
                at = pl.ds(pl.multiple_of(block * 8, 8), 8)
                fraction = fraction_ref[m1, at, :]
                for tap in range(8):
                    ratio = (float(tap - 3) - fraction) / 4.0
                    inner = jnp.maximum(1.0 - ratio * ratio, 0.0)
                    total = jnp.full_like(inner, coefficients[40])
                    for order in range(39, -1, -1):
                        total = total * inner + coefficients[order]
                    taps[tap, PAD + m1, at, :] = total

        def keep(tap, row, value):
            taps[tap, row] = value

        def keep_shift(row, value):
            shifts[row] = value

        @pl.loop(0, 8)
        def _(tap):
            extend(lambda row: taps[tap, row], functools.partial(keep, tap))

        extend(lambda row: shifts[row], keep_shift)

    table, _ = windows()
    for block in range(BLOCKS):
        at = pl.ds(8 * block, 8)
        start, offsets = table[block]
        for index, e in enumerate(offsets):
            row = q1 - e + PAD
            shift = shifts[row, at, :]
            value = jnp.zeros((8, LANES), jnp.float32)
            for tap in range(8):
                value = jnp.where(shift == 2 * e + 3 - tap, taps[tap, row, at, :], value)
            out_ref[0, start + index] = value


def weights(codes, bins):
    _, entries = windows()
    pulse = jnp.arange(MINOR, dtype=jnp.int32)[:, None] + MINOR * jnp.arange(MAJOR, dtype=jnp.int32)[None, :]
    slow = (pulse - PULSES // 2)[:, :, None]
    numerator = 2 * slow * TONE
    denominator = TONE + codes[None, None, :]
    cell_floor = jnp.floor_divide(numerator, denominator)
    fraction = (numerator - cell_floor * denominator).astype(jnp.float32) / denominator.astype(jnp.float32)
    shift = cell_floor - 2 * slow
    whole = pl.BlockSpec((MINOR, MAJOR, LANES), lambda q: (0, 0, 0))
    spread = MINOR + 2 * PAD
    return pl.pallas_call(
        functools.partial(weight_body, bins),
        grid=(MINOR,),
        in_specs=[whole, whole],
        out_specs=pl.BlockSpec((1, entries, 8, LANES), lambda q: (q, 0, 0, 0)),
        out_shape=jax.ShapeDtypeStruct((MINOR, entries, 8, LANES), jnp.float32),
        scratch_shapes=[
            pltpu.VMEM((8, spread, MAJOR, LANES), jnp.float32),
            pltpu.VMEM((spread, MAJOR, LANES), jnp.int32),
        ],
        compiler_params=pltpu.CompilerParams(vmem_limit_bytes=56 * 2**20),
        cost_estimate=pl.CostEstimate(
            flops=100 * 2**20 * 8, bytes_accessed=64 * 2**20, transcendentals=0
        ),
        name="weights",
    )(shift, fraction)


def times(value, turn, size):
    real, imag = value
    turn %= size
    if turn == 0:
        return value
    if 4 * turn == size:
        return (imag, -real)
    if 2 * turn == size:
        return (-real, -imag)
    if 4 * turn == 3 * size:
        return (-imag, real)
    if (8 * turn) % size == 0:
        half = math.sqrt(0.5)
        kind = 8 * turn // size
        if kind == 1:
            return (half * (real + imag), half * (imag - real))
        if kind == 3:
            return (half * (imag - real), -half * (real + imag))
        if kind == 5:
            return (-half * (real + imag), half * (real - imag))
        return (half * (real - imag), half * (real + imag))
    cosine = math.cos(2.0 * math.pi * turn / size)
    sine = math.sin(2.0 * math.pi * turn / size)
    return (real * cosine + imag * sine, imag * cosine - real * sine)


def plus(one, two):
    return (one[0] + two[0], one[1] + two[1])


def minus(one, two):
    return (one[0] - two[0], one[1] - two[1])


def dft4(values):
    sum_a, dif_a = plus(values[0], values[2]), minus(values[0], values[2])
    sum_b, dif_b = plus(values[1], values[3]), minus(values[1], values[3])
    side = (dif_b[1], -dif_b[0])
    return [plus(sum_a, sum_b), plus(dif_a, side), minus(sum_a, sum_b), minus(dif_a, side)]


def dft16(load):
    columns = []
    for low in range(4):
        done = dft4([load(low + 4 * high) for high in range(4)])
        columns.append([times(done[k], low * k, 16) for k in range(4)])
    result = [None] * 16
    for k in range(4):
        done = dft4([columns[low][k] for low in range(4)])
        for high in range(4):
            result[k + 4 * high] = done[high]
    return result


def main_body(first, count, rows, bins, has_base, close, recv_ref, weight_ref, turn_ref, scale_ref, *rest):
    if has_base:
        rest = rest[1:]
    out_ref, spread, pairs, mids, tall, wide, sem = rest[:7]
    if close:
        weight_far, turn_far = weight_ref, turn_ref
        weight_ref, turn_ref, fetched = rest[7:]

        def fetch_weight(q):
            return pltpu.make_async_copy(weight_far.at[q], weight_ref.at[q], fetched.at[0, q])

        def fetch_turn(q):
            return pltpu.make_async_copy(turn_far.at[q], turn_ref.at[q], fetched.at[1, q])

        for q in range(MINOR):
            fetch_weight(q).start()
            fetch_turn(q).start()

    devices, depth = recv_ref.shape[0], recv_ref.shape[3] // MINOR

    def begin():
        for unit in range(count):
            for part in range(2):
                @pl.loop(0, MINOR)
                def _(m1):
                    for device in range(devices):
                        at = pl.ds(pl.multiple_of(m1 * depth, depth), depth)
                        spread[PAD + m1, part, unit, pl.ds(device * depth, depth), :] = recv_ref[device, unit, part, at, :]

                def keep(row, value):
                    spread[row, part, unit] = value

                extend(lambda row: spread[row, part, unit], keep)

    def combine(before):
        turn_at = before if close else 0
        dot = functools.partial(jnp.dot, preferred_element_type=jnp.float32)
        width = count * LANES
        for parity in range(2):
            full = pairs[parity]
            high = full.astype(jnp.bfloat16)
            low = (full - high.astype(jnp.float32)).astype(jnp.bfloat16)
            turn_high, turn_low = turn_ref[turn_at, parity, 0], turn_ref[turn_at, parity, 1]
            if count == 1:
                both = dot(turn_high, jnp.concatenate([high, low], 1))
                mids[before, parity] = both[:, :width] + (both[:, width:] + dot(turn_low, high))
            else:
                mids[before, parity] = dot(turn_high, high) + (dot(turn_high, low) + dot(turn_low, high))

    def step(q1):
        before = jnp.maximum(q1 - 1, 0)
        if close:
            fetch_weight(q1).wait()

            @pl.when(q1 != 1)
            def _():
                fetch_turn(before).wait()

        combine(before)
        weight_at = q1 if close else 0
        table, _ = windows()
        first_parity = lax.broadcasted_iota(jnp.int32, (8, LANES), 1) // bins % 2 == 0
        for block in range(BLOCKS):
            start, offsets = table[block]
            sums = {}
            for index, e in enumerate(offsets):
                weight = weight_ref[weight_at, start + index]
                weight = (weight, pltpu.roll(weight, bins, 1))
                row = q1 - e + PAD
                for part in range(2):
                    for unit in range(count):
                        sample = spread[row, part, unit, pl.ds(8 * block, 8), :]
                        for turn in range(2):
                            term = weight[turn] * sample
                            key = (turn, part, unit)
                            sums[key] = sums[key] + term if key in sums else term
            for part in range(2):
                for unit in range(count):
                    own, other = sums[0, part, unit], sums[1, part, unit]
                    at = (pl.ds(part * MAJOR + 8 * block, 8), pl.ds(unit * LANES, LANES))
                    pairs[(0,) + at] = jnp.where(first_parity, own, other)
                    pairs[(1,) + at] = jnp.where(first_parity, other, own)

    span = PULSES // CUTS

    def leave(unit, part, cut):
        at = pl.ds(pl.multiple_of(cut * span, span), span)
        return pltpu.make_async_copy(
            wide.at[part, :, :, at],
            out_ref.at[part, pl.ds((first + unit) * rows, rows), :, at],
            sem.at[unit, part, cut],
        )

    def end():
        if close:
            fetch_turn(MINOR - 1).wait()
        combine(MINOR - 1)
        for unit in range(count):
            across = pl.ds(unit * LANES, LANES)

            @pl.loop(0, BLOCKS)
            def _(block):
                def load(parity, q):
                    return tuple(
                        mids[q, parity, pl.ds(pl.multiple_of(part * MAJOR + 8 * block, 8), 8), across]
                        for part in range(2)
                    )

                even = dft16(functools.partial(load, 0))
                odd = dft16(functools.partial(load, 1))
                for n1 in range(16):
                    k = n1 - 8
                    value = plus(even[k % 16], times(odd[k % 16], k, 32))
                    for part in range(2):
                        tall[part, n1, pl.ds(pl.multiple_of(8 * block, 8), 8), :] = value[part]

            for part in range(2):
                @pl.loop(0, CUTS)
                def _(cut):
                    if unit:
                        leave(unit - 1, part, cut).wait()
                    for member in range(16 // CUTS):
                        n1 = cut * (16 // CUTS) + member
                        at = pl.ds(pl.multiple_of(n1 * LANES, LANES), LANES)
                        turned = jnp.transpose(tall[part, n1]) * scale_ref[pl.ds(0, 1), at]
                        for row in range(rows):
                            wide[part, row, :, at] = turned[row * bins : (row + 1) * bins]
                    leave(unit, part, cut).start()
        for part in range(2):
            for cut in range(CUTS):
                leave(count - 1, part, cut).wait()

    if close:
        begin()
        pl.loop(0, MINOR)(step)
        end()
    else:
        now = pl.program_id(0)
        pl.when(now == 0)(begin)
        pl.when(now < MINOR)(lambda: step(now))
        pl.when(now == MINOR)(end)


def finish(recv, weight, turn, scale, base, first, total):
    devices, count = recv.shape[0], recv.shape[1]
    bins = BINS // devices
    rows = LANES // bins
    _, entries = windows()
    close = count == 1
    if close:
        in_specs = [
            pl.BlockSpec(memory_space=pltpu.VMEM),
            pl.BlockSpec(memory_space=pl.ANY),
            pl.BlockSpec(memory_space=pl.ANY),
        ]
    else:
        in_specs = [
            pl.BlockSpec(recv.shape, lambda q: (0, 0, 0, 0, 0), pipeline_mode=pl.Buffered(1)),
            pl.BlockSpec((1, entries, 8, LANES), lambda q: (jnp.minimum(q, MINOR - 1), 0, 0, 0)),
            pl.BlockSpec((1, 2, 2, 2 * MAJOR, 2 * MAJOR), lambda q: (jnp.maximum(q - 1, 0), 0, 0, 0, 0)),
        ]
    in_specs.append(pl.BlockSpec((1, PULSES), (lambda: (0, 0)) if close else (lambda q: (0, 0))))
    args = [recv, weight, turn, scale]
    if base is not None:
        in_specs.append(pl.BlockSpec(memory_space=pl.ANY))
        args.append(base)
    ahead = []
    if close:
        ahead = [
            pltpu.VMEM(weight.shape, jnp.float32),
            pltpu.VMEM(turn.shape, jnp.bfloat16),
            pltpu.SemaphoreType.DMA((2, MINOR)),
        ]
    return pl.pallas_call(
        functools.partial(main_body, first, count, rows, bins, base is not None, close),
        grid=() if close else (MINOR + 1,),
        in_specs=in_specs,
        out_specs=pl.BlockSpec(memory_space=pl.ANY),
        out_shape=jax.ShapeDtypeStruct((2, total, bins, PULSES), jnp.float32),
        scratch_shapes=[
            pltpu.VMEM((MINOR + 2 * PAD, 2, count, MAJOR, LANES), jnp.float32),
            pltpu.VMEM((2, 2 * MAJOR, count * LANES), jnp.float32),
            pltpu.VMEM((MINOR, 2, 2 * MAJOR, count * LANES), jnp.float32),
            pltpu.VMEM((2, 16, MAJOR, LANES), jnp.float32),
            pltpu.VMEM((2, rows, bins, PULSES), jnp.float32),
            pltpu.SemaphoreType.DMA((count, 2, CUTS)),
        ]
        + ahead,
        input_output_aliases={} if base is None else {4: 0},
        compiler_params=pltpu.CompilerParams(vmem_limit_bytes=(48 if close else 58) * 2**20),
        cost_estimate=pl.CostEstimate(
            flops=count * 32 * 6 * 256 * 256 * 128, bytes_accessed=(36 + 4 * count) * 2**20, transcendentals=0
        ),
        name="finish",
    )(*args)


def on_device(devices, echo, spectral_shift_units):
    bins = BINS // devices
    rows = LANES // bins
    lead = echo.shape[1] * echo.shape[2]
    flat = echo.reshape((2, lead) + echo.shape[3:])
    units = lead // rows
    cuts = (0, units - 1, units) if units > 1 else (0, units)
    codes = lax.dynamic_slice_in_dim(spectral_shift_units, lax.axis_index("pulse") * bins, bins, 0)
    sent = [pack(flat, first, last - first, devices) for first, last in zip(cuts[:-1], cuts[1:])]
    weight = weights(jnp.tile(codes, rows), bins)
    received = [lax.all_to_all(sent[0], "pulse", 0, 0, tiled=True)]
    for later in sent[1:]:
        later, weight = lax.optimization_barrier((later, weight))
        received.append(lax.all_to_all(later, "pulse", 0, 0, tiled=True))
    turn = jnp.asarray(turns())
    scale = correction(PULSES).reshape(1, PULSES)
    out = None
    for first, recv in zip(cuts[:-1], received):
        out = finish(recv, weight, turn, scale, out, first, lead)
    return out.reshape(echo.shape[:3] + (bins, PULSES))


def solution(mesh):
    placed = (P(None, "grp", None, "pulse", None), P())
    return jax.shard_map(
        functools.partial(on_device, mesh.shape["pulse"]),
        mesh=mesh,
        in_specs=placed,
        out_specs=P(None, "grp", None, "pulse", None),
        check_vma=False,
    )
```

```python
import functools
import math

import jax
import jax.numpy as jnp
import numpy as np
from jax import lax
from jax.experimental import pallas as pl
from jax.experimental.pallas import tpu as pltpu
from jax.sharding import PartitionSpec as P

PULSES = 2048
BINS = 1024
TONE = 16 * PULSES
CODE_MAX = PULSES // 8
MINOR = 16
MAJOR = PULSES // MINOR
PAD = 10
BLOCKS = MAJOR // 8
LANES = 128
AHEAD = 6
CUTS = 2

BETA_KB = math.pi * math.sqrt(35.2)


def bessel_zero(value):
    quarter = value * value * 0.25
    term = jnp.ones_like(value)
    total = jnp.ones_like(value)
    for order in range(1, 41):
        term = term * quarter / float(order * order)
        total = total + term
    return total


def correction(number_of_echoes):
    grid_size = 2 * number_of_echoes
    doppler_bin_index = jnp.arange(number_of_echoes, dtype=jnp.int32) - number_of_echoes // 2
    phase = math.pi * 8.0 / grid_size * doppler_bin_index.astype(jnp.float32)
    root = jnp.sqrt(BETA_KB * BETA_KB - phase * phase)
    parity = (1 - 2 * (doppler_bin_index % 2)).astype(jnp.float32)
    peak = bessel_zero(BETA_KB * jnp.ones((), jnp.float32))
    return parity * peak * root / (8.0 * jnp.sinh(root)) / math.sqrt(number_of_echoes)


@functools.lru_cache(None)
def windows():
    pulse = np.arange(PULSES)
    numerator = 2 * (pulse - PULSES // 2) * TONE
    ends = np.stack([numerator // (TONE + code) - 2 * (pulse - PULSES // 2) for code in (-CODE_MAX, CODE_MAX)])
    low, high = ends.min(0) - 3, ends.max(0) + 4
    out, start = [], 0
    for block in range(BLOCKS):
        pairs = np.arange(128 * block, 128 * (block + 1))
        offsets = []
        for e in range(-PAD, PAD + 1):
            source = (pairs - e) % PULSES
            if np.any((low[source] <= 2 * e + 1) & (2 * e <= high[source])):
                offsets.append(e)
        out.append((start, tuple(offsets)))
        start += len(offsets)
    return tuple(out), start


@functools.lru_cache(None)
def series():
    terms = [1.0]
    for order in range(1, 41):
        terms.append(terms[-1] * (BETA_KB * BETA_KB / 4.0) / float(order * order))
    peak = math.fsum(terms)
    return tuple(term / peak for term in terms)


@functools.lru_cache(None)
def turns():
    r = np.arange(2 * MINOR)[:, None, None]
    n2 = np.arange(MAJOR)[None, :, None]
    q2 = np.arange(MAJOR)[None, None, :]
    angle = 2.0 * math.pi / (2 * PULSES) * ((32 * q2 + r) * n2 % (2 * PULSES))
    cosine, sine = np.cos(angle), np.sin(angle)
    full = np.concatenate(
        [np.concatenate([cosine, sine], 2), np.concatenate([-sine, cosine], 2)], 1
    )
    high = full.astype(jnp.bfloat16)
    low = (full - high.astype(np.float64)).astype(jnp.bfloat16)
    both = np.stack([high, low], 1)
    return both.reshape(MINOR, 2, 2, 2 * MAJOR, 2 * MAJOR)


def pack_body(rows, bins, first, pieces, echo_ref, out_ref, taken, ready, taking, leaving):
    held = echo_ref.shape[2]
    depth = held // MINOR
    lane = lax.broadcasted_iota(jnp.int32, (8, LANES), 1) // bins

    def take(piece):
        source = echo_ref.at[piece % 2, pl.ds((first + piece // 2) * rows, rows)]
        return pltpu.make_async_copy(source, taken.at[piece], taking.at[piece])

    def leave(piece):
        return pltpu.make_async_copy(ready.at[piece], out_ref.at[:, piece // 2, piece % 2], leaving.at[piece])

    for piece in range(min(AHEAD, pieces)):
        take(piece).start()

    @pl.loop(0, pieces)
    def _(piece):
        take(piece).wait()

        @pl.when(piece + AHEAD < pieces)
        def _():
            take(piece + AHEAD).start()

        for column in range(BINS // LANES):
            for group in range(held // 8):
                values = [
                    taken[piece, row, pl.ds(8 * group, 8), pl.ds(column * LANES, LANES)] for row in range(rows)
                ]
                to = pl.ds(8 * group % MINOR * depth + 8 * group // MINOR, 8, stride=depth)
                for dest in range(rows):
                    value = None
                    for row in range(rows):
                        turn = (row - dest) * bins % LANES
                        moved = pltpu.roll(values[row], turn, 1) if turn else values[row]
                        value = moved if value is None else jnp.where(lane == row, moved, value)
                    ready[piece, column * rows + dest, to, :] = value
        leave(piece).start()

    @pl.loop(0, pieces)
    def _(piece):
        leave(piece).wait()


def pack(echo, first, count, devices):
    bins = BINS // devices
    rows = LANES // bins
    held = echo.shape[2]
    pieces = 2 * count
    return pl.pallas_call(
        functools.partial(pack_body, rows, bins, first, pieces),
        in_specs=[pl.BlockSpec(memory_space=pl.ANY)],
        out_specs=pl.BlockSpec(memory_space=pl.ANY),
        out_shape=jax.ShapeDtypeStruct((devices, count, 2, held, LANES), jnp.float32),
        scratch_shapes=[
            pltpu.VMEM((pieces, rows, held, BINS), jnp.float32),
            pltpu.VMEM((pieces, devices, held, LANES), jnp.float32),
            pltpu.SemaphoreType.DMA((pieces,)),
            pltpu.SemaphoreType.DMA((pieces,)),
        ],
        compiler_params=pltpu.CompilerParams(vmem_limit_bytes=56 * 2**20),
        cost_estimate=pl.CostEstimate(
            flops=0, bytes_accessed=16 * devices * count * held * LANES, transcendentals=0
        ),
        name="pack",
    )(echo)


def extend(ref, store):
    for m1 in range(MINOR - PAD, MINOR):
        store(m1 - MINOR + PAD, pltpu.roll(ref(m1 + PAD), 1, 0))
    for m1 in range(PAD):
        store(m1 + MINOR + PAD, pltpu.roll(ref(m1 + PAD), MAJOR - 1, 0))


def weight_body(bins, shift_ref, fraction_ref, out_ref, taps, shifts):
    q1 = pl.program_id(0)
    parity = lax.broadcasted_iota(jnp.int32, (MAJOR, LANES), 1) // bins % 2

    @pl.when(q1 == 0)
    def _():
        coefficients = series()

        @pl.loop(0, MINOR)
        def _(m1):
            shifts[PAD + m1] = shift_ref[m1] - parity

            @pl.loop(0, BLOCKS)
            def _(block):
                at = pl.ds(pl.multiple_of(block * 8, 8), 8)
                fraction = fraction_ref[m1, at, :]
                for tap in range(8):
                    ratio = (float(tap - 3) - fraction) / 4.0
                    inner = jnp.maximum(1.0 - ratio * ratio, 0.0)
                    total = jnp.full_like(inner, coefficients[40])
                    for order in range(39, -1, -1):
                        total = total * inner + coefficients[order]
                    taps[tap, PAD + m1, at, :] = total

        def keep(tap, row, value):
            taps[tap, row] = value

        def keep_shift(row, value):
            shifts[row] = value

        @pl.loop(0, 8)
        def _(tap):
            extend(lambda row: taps[tap, row], functools.partial(keep, tap))

        extend(lambda row: shifts[row], keep_shift)

    table, _ = windows()
    for block in range(BLOCKS):
        at = pl.ds(8 * block, 8)
        start, offsets = table[block]
        for index, e in enumerate(offsets):
            row = q1 - e + PAD
            shift = shifts[row, at, :]
            value = jnp.zeros((8, LANES), jnp.float32)
            for tap in range(8):
                value = jnp.where(shift == 2 * e + 3 - tap, taps[tap, row, at, :], value)
            out_ref[0, start + index] = value


def weights(codes, bins):
    _, entries = windows()
    pulse = jnp.arange(MINOR, dtype=jnp.int32)[:, None] + MINOR * jnp.arange(MAJOR, dtype=jnp.int32)[None, :]
    slow = (pulse - PULSES // 2)[:, :, None]
    numerator = 2 * slow * TONE
    denominator = TONE + codes[None, None, :]
    cell_floor = jnp.floor_divide(numerator, denominator)
    fraction = (numerator - cell_floor * denominator).astype(jnp.float32) / denominator.astype(jnp.float32)
    shift = cell_floor - 2 * slow
    whole = pl.BlockSpec((MINOR, MAJOR, LANES), lambda q: (0, 0, 0))
    spread = MINOR + 2 * PAD
    return pl.pallas_call(
        functools.partial(weight_body, bins),
        grid=(MINOR,),
        in_specs=[whole, whole],
        out_specs=pl.BlockSpec((1, entries, 8, LANES), lambda q: (q, 0, 0, 0)),
        out_shape=jax.ShapeDtypeStruct((MINOR, entries, 8, LANES), jnp.float32),
        scratch_shapes=[
            pltpu.VMEM((8, spread, MAJOR, LANES), jnp.float32),
            pltpu.VMEM((spread, MAJOR, LANES), jnp.int32),
        ],
        compiler_params=pltpu.CompilerParams(vmem_limit_bytes=56 * 2**20),
        cost_estimate=pl.CostEstimate(
            flops=100 * 2**20 * 8, bytes_accessed=64 * 2**20, transcendentals=0
        ),
        name="weights",
    )(shift, fraction)


def times(value, turn, size):
    real, imag = value
    turn %= size
    if turn == 0:
        return value
    if 4 * turn == size:
        return (imag, -real)
    if 2 * turn == size:
        return (-real, -imag)
    if 4 * turn == 3 * size:
        return (-imag, real)
    if (8 * turn) % size == 0:
        half = math.sqrt(0.5)
        kind = 8 * turn // size
        if kind == 1:
            return (half * (real + imag), half * (imag - real))
        if kind == 3:
            return (half * (imag - real), -half * (real + imag))
        if kind == 5:
            return (-half * (real + imag), half * (real - imag))
        return (half * (real - imag), half * (real + imag))
    cosine = math.cos(2.0 * math.pi * turn / size)
    sine = math.sin(2.0 * math.pi * turn / size)
    return (real * cosine + imag * sine, imag * cosine - real * sine)


def plus(one, two):
    return (one[0] + two[0], one[1] + two[1])


def minus(one, two):
    return (one[0] - two[0], one[1] - two[1])


def dft4(values):
    sum_a, dif_a = plus(values[0], values[2]), minus(values[0], values[2])
    sum_b, dif_b = plus(values[1], values[3]), minus(values[1], values[3])
    side = (dif_b[1], -dif_b[0])
    return [plus(sum_a, sum_b), plus(dif_a, side), minus(sum_a, sum_b), minus(dif_a, side)]


def dft16(load):
    columns = []
    for low in range(4):
        done = dft4([load(low + 4 * high) for high in range(4)])
        columns.append([times(done[k], low * k, 16) for k in range(4)])
    result = [None] * 16
    for k in range(4):
        done = dft4([columns[low][k] for low in range(4)])
        for high in range(4):
            result[k + 4 * high] = done[high]
    return result


def main_body(first, count, rows, bins, has_base, close, recv_ref, weight_ref, turn_ref, scale_ref, *rest):
    if has_base:
        rest = rest[1:]
    out_ref, spread, pairs, mids, tall, wide, sem = rest[:7]
    if close:
        weight_far, turn_far = weight_ref, turn_ref
        weight_ref, turn_ref, fetched = rest[7:]

        def fetch_weight(q):
            return pltpu.make_async_copy(weight_far.at[q], weight_ref.at[q], fetched.at[0, q])

        def fetch_turn(q):
            return pltpu.make_async_copy(turn_far.at[q], turn_ref.at[q], fetched.at[1, q])

        for q in range(MINOR):
            fetch_weight(q).start()
            fetch_turn(q).start()

    devices, depth = recv_ref.shape[0], recv_ref.shape[3] // MINOR

    def begin():
        for unit in range(count):
            for part in range(2):
                @pl.loop(0, MINOR)
                def _(m1):
                    for device in range(devices):
                        at = pl.ds(pl.multiple_of(m1 * depth, depth), depth)
                        spread[PAD + m1, part, unit, pl.ds(device * depth, depth), :] = recv_ref[device, unit, part, at, :]

                def keep(row, value):
                    spread[row, part, unit] = value

                extend(lambda row: spread[row, part, unit], keep)

    def combine(before):
        turn_at = before if close else 0
        dot = functools.partial(jnp.dot, preferred_element_type=jnp.float32)
        for parity in range(2):
            full = pairs[parity]
            high = full.astype(jnp.bfloat16)
            low = (full - high.astype(jnp.float32)).astype(jnp.bfloat16)
            turn_high, turn_low = turn_ref[turn_at, parity, 0], turn_ref[turn_at, parity, 1]
            if count == 1:
                across = functools.partial(
                    lax.dot_general,
                    dimension_numbers=(((0,), (1,)), ((), ())),
                    preferred_element_type=jnp.float32,
                )
                both = across(jnp.concatenate([high, low], 1), turn_high)
                mids[before, parity] = both[:LANES] + (both[LANES:] + across(high, turn_low))
            else:
                mids[before, parity] = dot(turn_high, high) + (dot(turn_high, low) + dot(turn_low, high))

    def step(q1):
        before = jnp.maximum(q1 - 1, 0)
        if close:
            fetch_weight(q1).wait()

            @pl.when(q1 != 1)
            def _():
                fetch_turn(before).wait()

        combine(before)
        weight_at = q1 if close else 0
        table, _ = windows()
        first_parity = lax.broadcasted_iota(jnp.int32, (8, LANES), 1) // bins % 2 == 0
        for block in range(BLOCKS):
            start, offsets = table[block]
            sums = {}
            for index, e in enumerate(offsets):
                weight = weight_ref[weight_at, start + index]
                weight = (weight, pltpu.roll(weight, bins, 1))
                row = q1 - e + PAD
                for part in range(2):
                    for unit in range(count):
                        sample = spread[row, part, unit, pl.ds(8 * block, 8), :]
                        for turn in range(2):
                            term = weight[turn] * sample
                            key = (turn, part, unit)
                            sums[key] = sums[key] + term if key in sums else term
            for part in range(2):
                for unit in range(count):
                    own, other = sums[0, part, unit], sums[1, part, unit]
                    at = (pl.ds(part * MAJOR + 8 * block, 8), pl.ds(unit * LANES, LANES))
                    pairs[(0,) + at] = jnp.where(first_parity, own, other)
                    pairs[(1,) + at] = jnp.where(first_parity, other, own)

    span = PULSES // CUTS

    def leave(unit, part, cut):
        at = pl.ds(pl.multiple_of(cut * span, span), span)
        return pltpu.make_async_copy(
            wide.at[part, :, :, at],
            out_ref.at[part, pl.ds((first + unit) * rows, rows), :, at],
            sem.at[unit, part, cut],
        )

    def depart(row):
        return pltpu.make_async_copy(
            wide.at[:, row], out_ref.at[:, first * rows + row], sem.at[0, 0, row % CUTS]
        )

    def end_close():
        fetch_turn(MINOR - 1).wait()
        combine(MINOR - 1)
        for row in range(rows):
            if row >= CUTS:
                depart(row - CUTS).wait()

            @pl.loop(0, bins // 8, unroll=2)
            def _(group):
                here = pl.ds(pl.multiple_of(group * 8, 8), 8)

                def load(parity, q):
                    return tuple(
                        mids[q, parity, pl.ds(pl.multiple_of(row * bins + group * 8, 8), 8), pl.ds(part * LANES, LANES)]
                        for part in range(2)
                    )

                even = dft16(functools.partial(load, 0))
                odd = dft16(functools.partial(load, 1))
                for n1 in range(16):
                    at = pl.ds(n1 * LANES, LANES)
                    value = plus(even[(n1 - 8) % 16], times(odd[(n1 - 8) % 16], n1 - 8, 32))
                    for part in range(2):
                        wide[part, row, here, at] = value[part] * scale_ref[pl.ds(0, 1), at]

            depart(row).start()
        for row in range(max(rows - CUTS, 0), rows):
            depart(row).wait()

    def end():
        combine(MINOR - 1)
        for unit in range(count):
            across = pl.ds(unit * LANES, LANES)

            @pl.loop(0, BLOCKS)
            def _(block):
                def load(parity, q):
                    return tuple(
                        mids[q, parity, pl.ds(pl.multiple_of(part * MAJOR + 8 * block, 8), 8), across]
                        for part in range(2)
                    )

                even = dft16(functools.partial(load, 0))
                odd = dft16(functools.partial(load, 1))
                for n1 in range(16):
                    k = n1 - 8
                    value = plus(even[k % 16], times(odd[k % 16], k, 32))
                    for part in range(2):
                        tall[part, n1, pl.ds(pl.multiple_of(8 * block, 8), 8), :] = value[part]

            for part in range(2):
                @pl.loop(0, CUTS)
                def _(cut):
                    if unit:
                        leave(unit - 1, part, cut).wait()
                    for member in range(16 // CUTS):
                        n1 = cut * (16 // CUTS) + member
                        at = pl.ds(pl.multiple_of(n1 * LANES, LANES), LANES)
                        turned = jnp.transpose(tall[part, n1]) * scale_ref[pl.ds(0, 1), at]
                        for row in range(rows):
                            wide[part, row, :, at] = turned[row * bins : (row + 1) * bins]
                    leave(unit, part, cut).start()
        for part in range(2):
            for cut in range(CUTS):
                leave(count - 1, part, cut).wait()

    if close:
        begin()
        pl.loop(0, MINOR)(step)
        end_close()
    else:
        now = pl.program_id(0)
        pl.when(now == 0)(begin)
        pl.when(now < MINOR)(lambda: step(now))
        pl.when(now == MINOR)(end)


def finish(recv, weight, turn, scale, base, first, total):
    devices, count = recv.shape[0], recv.shape[1]
    bins = BINS // devices
    rows = LANES // bins
    _, entries = windows()
    close = count == 1
    if close:
        in_specs = [
            pl.BlockSpec(memory_space=pltpu.VMEM),
            pl.BlockSpec(memory_space=pl.ANY),
            pl.BlockSpec(memory_space=pl.ANY),
        ]
    else:
        in_specs = [
            pl.BlockSpec(recv.shape, lambda q: (0, 0, 0, 0, 0), pipeline_mode=pl.Buffered(1)),
            pl.BlockSpec((1, entries, 8, LANES), lambda q: (jnp.minimum(q, MINOR - 1), 0, 0, 0)),
            pl.BlockSpec((1, 2, 2, 2 * MAJOR, 2 * MAJOR), lambda q: (jnp.maximum(q - 1, 0), 0, 0, 0, 0)),
        ]
    in_specs.append(pl.BlockSpec((1, PULSES), (lambda: (0, 0)) if close else (lambda q: (0, 0))))
    args = [recv, weight, turn, scale]
    if base is not None:
        in_specs.append(pl.BlockSpec(memory_space=pl.ANY))
        args.append(base)
    ahead = []
    if close:
        ahead = [
            pltpu.VMEM(weight.shape, jnp.float32),
            pltpu.VMEM(turn.shape, jnp.bfloat16),
            pltpu.SemaphoreType.DMA((2, MINOR)),
        ]
    return pl.pallas_call(
        functools.partial(main_body, first, count, rows, bins, base is not None, close),
        grid=() if close else (MINOR + 1,),
        in_specs=in_specs,
        out_specs=pl.BlockSpec(memory_space=pl.ANY),
        out_shape=jax.ShapeDtypeStruct((2, total, bins, PULSES), jnp.float32),
        scratch_shapes=[
            pltpu.VMEM((MINOR + 2 * PAD, 2, count, MAJOR, LANES), jnp.float32),
            pltpu.VMEM((2, 2 * MAJOR, count * LANES), jnp.float32),
            pltpu.VMEM((MINOR, 2) + ((LANES, 2 * MAJOR) if close else (2 * MAJOR, count * LANES)), jnp.float32),
            pltpu.VMEM((2, 16, MAJOR, LANES), jnp.float32),
            pltpu.VMEM((2, rows, bins, PULSES), jnp.float32),
            pltpu.SemaphoreType.DMA((count, 2, CUTS)),
        ]
        + ahead,
        input_output_aliases={} if base is None else {4: 0},
        compiler_params=pltpu.CompilerParams(vmem_limit_bytes=(48 if close else 58) * 2**20),
        cost_estimate=pl.CostEstimate(
            flops=count * 32 * 6 * 256 * 256 * 128, bytes_accessed=(36 + 4 * count) * 2**20, transcendentals=0
        ),
        name="finish",
    )(*args)


def on_device(devices, echo, spectral_shift_units):
    bins = BINS // devices
    rows = LANES // bins
    lead = echo.shape[1] * echo.shape[2]
    flat = echo.reshape((2, lead) + echo.shape[3:])
    units = lead // rows
    cuts = (0, units - 1, units) if units > 1 else (0, units)
    codes = lax.dynamic_slice_in_dim(spectral_shift_units, lax.axis_index("pulse") * bins, bins, 0)
    sent = [pack(flat, first, last - first, devices) for first, last in zip(cuts[:-1], cuts[1:])]
    weight = weights(jnp.tile(codes, rows), bins)
    received = [lax.all_to_all(sent[0], "pulse", 0, 0, tiled=True)]
    for later in sent[1:]:
        later, weight = lax.optimization_barrier((later, weight))
        received.append(lax.all_to_all(later, "pulse", 0, 0, tiled=True))
    turn = jnp.asarray(turns())
    scale = correction(PULSES).reshape(1, PULSES)
    out = None
    for first, recv in zip(cuts[:-1], received):
        out = finish(recv, weight, turn, scale, out, first, lead)
    return out.reshape(echo.shape[:3] + (bins, PULSES))


def solution(mesh):
    placed = (P(None, "grp", None, "pulse", None), P())
    return jax.shard_map(
        functools.partial(on_device, mesh.shape["pulse"]),
        mesh=mesh,
        in_specs=placed,
        out_specs=P(None, "grp", None, "pulse", None),
        check_vma=False,
    )
```

```python
import functools
import math

import jax
import jax.numpy as jnp
import numpy as np
from jax import lax
from jax.experimental import pallas as pl
from jax.experimental.pallas import tpu as pltpu
from jax.sharding import PartitionSpec as P

PULSES = 2048
BINS = 1024
TONE = 16 * PULSES
CODE_MAX = PULSES // 8
MINOR = 16
MAJOR = PULSES // MINOR
PAD = 10
BLOCKS = MAJOR // 8
LANES = 128
AHEAD = 6
CUTS = 2

BETA_KB = math.pi * math.sqrt(35.2)


def bessel_zero(value):
    quarter = value * value * 0.25
    term = jnp.ones_like(value)
    total = jnp.ones_like(value)
    for order in range(1, 41):
        term = term * quarter / float(order * order)
        total = total + term
    return total


def correction(number_of_echoes):
    grid_size = 2 * number_of_echoes
    doppler_bin_index = jnp.arange(number_of_echoes, dtype=jnp.int32) - number_of_echoes // 2
    phase = math.pi * 8.0 / grid_size * doppler_bin_index.astype(jnp.float32)
    root = jnp.sqrt(BETA_KB * BETA_KB - phase * phase)
    parity = (1 - 2 * (doppler_bin_index % 2)).astype(jnp.float32)
    peak = bessel_zero(BETA_KB * jnp.ones((), jnp.float32))
    return parity * peak * root / (8.0 * jnp.sinh(root)) / math.sqrt(number_of_echoes)


@functools.lru_cache(None)
def windows():
    pulse = np.arange(PULSES)
    numerator = 2 * (pulse - PULSES // 2) * TONE
    ends = np.stack([numerator // (TONE + code) - 2 * (pulse - PULSES // 2) for code in (-CODE_MAX, CODE_MAX)])
    low, high = ends.min(0) - 3, ends.max(0) + 4
    out, start = [], 0
    for block in range(BLOCKS):
        pairs = np.arange(128 * block, 128 * (block + 1))
        offsets = []
        for e in range(-PAD, PAD + 1):
            source = (pairs - e) % PULSES
            if np.any((low[source] <= 2 * e + 1) & (2 * e <= high[source])):
                offsets.append(e)
        out.append((start, tuple(offsets)))
        start += len(offsets)
    return tuple(out), start


@functools.lru_cache(None)
def series():
    terms = [1.0]
    for order in range(1, 41):
        terms.append(terms[-1] * (BETA_KB * BETA_KB / 4.0) / float(order * order))
    peak = math.fsum(terms)
    return tuple(term / peak for term in terms)


@functools.lru_cache(None)
def turns():
    r = np.arange(2 * MINOR)[:, None, None]
    n2 = np.arange(MAJOR)[None, :, None]
    q2 = np.arange(MAJOR)[None, None, :]
    angle = 2.0 * math.pi / (2 * PULSES) * ((32 * q2 + r) * n2 % (2 * PULSES))
    cosine, sine = np.cos(angle), np.sin(angle)
    full = np.concatenate(
        [np.concatenate([cosine, sine], 2), np.concatenate([-sine, cosine], 2)], 1
    )
    high = full.astype(jnp.bfloat16)
    low = (full - high.astype(np.float64)).astype(jnp.bfloat16)
    both = np.stack([high, low], 1)
    return both.reshape(MINOR, 2, 2, 2 * MAJOR, 2 * MAJOR)


def pack_body(rows, bins, first, pieces, echo_ref, out_ref, taken, ready, taking, leaving):
    held = echo_ref.shape[2]
    depth = held // MINOR
    lane = lax.broadcasted_iota(jnp.int32, (8, LANES), 1) // bins

    def take(piece):
        source = echo_ref.at[piece % 2, pl.ds((first + piece // 2) * rows, rows)]
        return pltpu.make_async_copy(source, taken.at[piece], taking.at[piece])

    def leave(piece):
        return pltpu.make_async_copy(ready.at[piece], out_ref.at[:, piece // 2, piece % 2], leaving.at[piece])

    for piece in range(min(AHEAD, pieces)):
        take(piece).start()

    @pl.loop(0, pieces)
    def _(piece):
        take(piece).wait()

        @pl.when(piece + AHEAD < pieces)
        def _():
            take(piece + AHEAD).start()

        for column in range(BINS // LANES):
            for group in range(held // 8):
                values = [
                    taken[piece, row, pl.ds(8 * group, 8), pl.ds(column * LANES, LANES)] for row in range(rows)
                ]
                to = pl.ds(8 * group % MINOR * depth + 8 * group // MINOR, 8, stride=depth)
                for dest in range(rows):
                    value = None
                    for row in range(rows):
                        turn = (row - dest) * bins % LANES
                        moved = pltpu.roll(values[row], turn, 1) if turn else values[row]
                        value = moved if value is None else jnp.where(lane == row, moved, value)
                    ready[piece, column * rows + dest, to, :] = value
        leave(piece).start()

    @pl.loop(0, pieces)
    def _(piece):
        leave(piece).wait()


def pack(echo, first, count, devices):
    bins = BINS // devices
    rows = LANES // bins
    held = echo.shape[2]
    pieces = 2 * count
    return pl.pallas_call(
        functools.partial(pack_body, rows, bins, first, pieces),
        in_specs=[pl.BlockSpec(memory_space=pl.ANY)],
        out_specs=pl.BlockSpec(memory_space=pl.ANY),
        out_shape=jax.ShapeDtypeStruct((devices, count, 2, held, LANES), jnp.float32),
        scratch_shapes=[
            pltpu.VMEM((pieces, rows, held, BINS), jnp.float32),
            pltpu.VMEM((pieces, devices, held, LANES), jnp.float32),
            pltpu.SemaphoreType.DMA((pieces,)),
            pltpu.SemaphoreType.DMA((pieces,)),
        ],
        compiler_params=pltpu.CompilerParams(vmem_limit_bytes=56 * 2**20),
        cost_estimate=pl.CostEstimate(
            flops=0, bytes_accessed=16 * devices * count * held * LANES, transcendentals=0
        ),
        name="pack",
    )(echo)


def extend(ref, store):
    for m1 in range(MINOR - PAD, MINOR):
        store(m1 - MINOR + PAD, pltpu.roll(ref(m1 + PAD), 1, 0))
    for m1 in range(PAD):
        store(m1 + MINOR + PAD, pltpu.roll(ref(m1 + PAD), MAJOR - 1, 0))


def weight_body(bins, shift_ref, fraction_ref, out_ref, taps, shifts):
    q1 = pl.program_id(0)
    parity = lax.broadcasted_iota(jnp.int32, (MAJOR, LANES), 1) // bins % 2

    @pl.when(q1 == 0)
    def _():
        coefficients = series()

        @pl.loop(0, MINOR)
        def _(m1):
            shifts[PAD + m1] = shift_ref[m1] - parity

            @pl.loop(0, BLOCKS)
            def _(block):
                at = pl.ds(pl.multiple_of(block * 8, 8), 8)
                fraction = fraction_ref[m1, at, :]
                for tap in range(8):
                    ratio = (float(tap - 3) - fraction) / 4.0
                    inner = jnp.maximum(1.0 - ratio * ratio, 0.0)
                    total = jnp.full_like(inner, coefficients[40])
                    for order in range(39, -1, -1):
                        total = total * inner + coefficients[order]
                    taps[tap, PAD + m1, at, :] = total

        def keep(tap, row, value):
            taps[tap, row] = value

        def keep_shift(row, value):
            shifts[row] = value

        @pl.loop(0, 8)
        def _(tap):
            extend(lambda row: taps[tap, row], functools.partial(keep, tap))

        extend(lambda row: shifts[row], keep_shift)

    table, _ = windows()
    for block in range(BLOCKS):
        at = pl.ds(8 * block, 8)
        start, offsets = table[block]
        for index, e in enumerate(offsets):
            row = q1 - e + PAD
            shift = shifts[row, at, :]
            value = jnp.zeros((8, LANES), jnp.float32)
            for tap in range(8):
                value = jnp.where(shift == 2 * e + 3 - tap, taps[tap, row, at, :], value)
            out_ref[0, start + index] = value


def weights(codes, bins):
    _, entries = windows()
    pulse = jnp.arange(MINOR, dtype=jnp.int32)[:, None] + MINOR * jnp.arange(MAJOR, dtype=jnp.int32)[None, :]
    slow = (pulse - PULSES // 2)[:, :, None]
    numerator = 2 * slow * TONE
    denominator = TONE + codes[None, None, :]
    cell_floor = jnp.floor_divide(numerator, denominator)
    fraction = (numerator - cell_floor * denominator).astype(jnp.float32) / denominator.astype(jnp.float32)
    shift = cell_floor - 2 * slow
    whole = pl.BlockSpec((MINOR, MAJOR, LANES), lambda q: (0, 0, 0))
    spread = MINOR + 2 * PAD
    return pl.pallas_call(
        functools.partial(weight_body, bins),
        grid=(MINOR,),
        in_specs=[whole, whole],
        out_specs=pl.BlockSpec((1, entries, 8, LANES), lambda q: (q, 0, 0, 0)),
        out_shape=jax.ShapeDtypeStruct((MINOR, entries, 8, LANES), jnp.float32),
        scratch_shapes=[
            pltpu.VMEM((8, spread, MAJOR, LANES), jnp.float32),
            pltpu.VMEM((spread, MAJOR, LANES), jnp.int32),
        ],
        compiler_params=pltpu.CompilerParams(vmem_limit_bytes=56 * 2**20),
        cost_estimate=pl.CostEstimate(
            flops=100 * 2**20 * 8, bytes_accessed=64 * 2**20, transcendentals=0
        ),
        name="weights",
    )(shift, fraction)


def times(value, turn, size):
    real, imag = value
    turn %= size
    if turn == 0:
        return value
    if 4 * turn == size:
        return (imag, -real)
    if 2 * turn == size:
        return (-real, -imag)
    if 4 * turn == 3 * size:
        return (-imag, real)
    if (8 * turn) % size == 0:
        half = math.sqrt(0.5)
        kind = 8 * turn // size
        if kind == 1:
            return (half * (real + imag), half * (imag - real))
        if kind == 3:
            return (half * (imag - real), -half * (real + imag))
        if kind == 5:
            return (-half * (real + imag), half * (real - imag))
        return (half * (real - imag), half * (real + imag))
    cosine = math.cos(2.0 * math.pi * turn / size)
    sine = math.sin(2.0 * math.pi * turn / size)
    return (real * cosine + imag * sine, imag * cosine - real * sine)


def plus(one, two):
    return (one[0] + two[0], one[1] + two[1])


def minus(one, two):
    return (one[0] - two[0], one[1] - two[1])


def dft4(values):
    sum_a, dif_a = plus(values[0], values[2]), minus(values[0], values[2])
    sum_b, dif_b = plus(values[1], values[3]), minus(values[1], values[3])
    side = (dif_b[1], -dif_b[0])
    return [plus(sum_a, sum_b), plus(dif_a, side), minus(sum_a, sum_b), minus(dif_a, side)]


def dft16(load):
    columns = []
    for low in range(4):
        done = dft4([load(low + 4 * high) for high in range(4)])
        columns.append([times(done[k], low * k, 16) for k in range(4)])
    result = [None] * 16
    for k in range(4):
        done = dft4([columns[low][k] for low in range(4)])
        for high in range(4):
            result[k + 4 * high] = done[high]
    return result


def main_body(first, count, rows, bins, has_base, close, recv_ref, weight_ref, turn_ref, scale_ref, *rest):
    if has_base:
        rest = rest[1:]
    out_ref, spread, pairs, mids, tall, wide, sem = rest[:7]
    if close:
        weight_far, turn_far = weight_ref, turn_ref
        weight_ref, turn_ref, fetched = rest[7:]

        def fetch_weight(q):
            return pltpu.make_async_copy(weight_far.at[q], weight_ref.at[q], fetched.at[0, q])

        def fetch_turn(q):
            return pltpu.make_async_copy(turn_far.at[q], turn_ref.at[q], fetched.at[1, q])

        for q in range(MINOR):
            fetch_weight(q).start()
            fetch_turn(q).start()

    devices, depth = recv_ref.shape[0], recv_ref.shape[3] // MINOR

    def begin():
        for unit in range(count):
            for part in range(2):
                @pl.loop(0, MINOR)
                def _(m1):
                    for device in range(devices):
                        at = pl.ds(pl.multiple_of(m1 * depth, depth), depth)
                        spread[PAD + m1, part, unit, pl.ds(device * depth, depth), :] = recv_ref[device, unit, part, at, :]

                def keep(row, value):
                    spread[row, part, unit] = value

                extend(lambda row: spread[row, part, unit], keep)

    def combine(before):
        turn_at = before if close else 0
        dot = functools.partial(jnp.dot, preferred_element_type=jnp.float32)
        for parity in range(2):
            full = pairs[parity]
            high = full.astype(jnp.bfloat16)
            low = (full - high.astype(jnp.float32)).astype(jnp.bfloat16)
            turn_high, turn_low = turn_ref[turn_at, parity, 0], turn_ref[turn_at, parity, 1]
            if count == 1:
                across = functools.partial(
                    lax.dot_general,
                    dimension_numbers=(((0,), (1,)), ((), ())),
                    preferred_element_type=jnp.float32,
                )
                both = across(jnp.concatenate([high, low], 1), turn_high)
                mids[before, parity] = both[:LANES] + (both[LANES:] + across(high, turn_low))
            else:
                mids[before, parity] = dot(turn_high, high) + (dot(turn_high, low) + dot(turn_low, high))

    def step(q1):
        before = jnp.maximum(q1 - 1, 0)
        if close:
            fetch_weight(q1).wait()

            @pl.when(q1 != 1)
            def _():
                fetch_turn(before).wait()

        combine(before)
        weight_at = q1 if close else 0
        table, _ = windows()
        first_parity = lax.broadcasted_iota(jnp.int32, (8, LANES), 1) // bins % 2 == 0
        for block in range(BLOCKS):
            start, offsets = table[block]
            sums = {}
            for index, e in enumerate(offsets):
                weight = weight_ref[weight_at, start + index]
                weight = (weight, pltpu.roll(weight, bins, 1))
                row = q1 - e + PAD
                for part in range(2):
                    for unit in range(count):
                        sample = spread[row, part, unit, pl.ds(8 * block, 8), :]
                        for turn in range(2):
                            term = weight[turn] * sample
                            key = (turn, part, unit)
                            sums[key] = sums[key] + term if key in sums else term
            for part in range(2):
                for unit in range(count):
                    own, other = sums[0, part, unit], sums[1, part, unit]
                    at = (pl.ds(part * MAJOR + 8 * block, 8), pl.ds(unit * LANES, LANES))
                    pairs[(0,) + at] = jnp.where(first_parity, own, other)
                    pairs[(1,) + at] = jnp.where(first_parity, other, own)

    span = PULSES // CUTS

    def leave(unit, part, cut):
        at = pl.ds(pl.multiple_of(cut * span, span), span)
        return pltpu.make_async_copy(
            wide.at[part, :, :, at],
            out_ref.at[part, pl.ds((first + unit) * rows, rows), :, at],
            sem.at[unit, part, cut],
        )

    def depart(row):
        return pltpu.make_async_copy(
            wide.at[:, row], out_ref.at[:, first * rows + row], sem.at[0, 0, row % CUTS]
        )

    def end_close():
        fetch_turn(MINOR - 1).wait()
        combine(MINOR - 1)
        for row in range(rows):
            if row >= CUTS:
                depart(row - CUTS).wait()

            @pl.loop(0, bins // 8, unroll=4)
            def _(group):
                here = pl.ds(pl.multiple_of(group * 8, 8), 8)

                def load(parity, q):
                    return tuple(
                        mids[q, parity, pl.ds(pl.multiple_of(row * bins + group * 8, 8), 8), pl.ds(part * LANES, LANES)]
                        for part in range(2)
                    )

                even = dft16(functools.partial(load, 0))
                odd = dft16(functools.partial(load, 1))
                for n1 in range(16):
                    at = pl.ds(n1 * LANES, LANES)
                    value = plus(even[(n1 - 8) % 16], times(odd[(n1 - 8) % 16], n1 - 8, 32))
                    for part in range(2):
                        wide[part, row, here, at] = value[part] * scale_ref[pl.ds(0, 1), at]

            depart(row).start()
        for row in range(max(rows - CUTS, 0), rows):
            depart(row).wait()

    def end():
        combine(MINOR - 1)
        for unit in range(count):
            across = pl.ds(unit * LANES, LANES)

            @pl.loop(0, BLOCKS)
            def _(block):
                def load(parity, q):
                    return tuple(
                        mids[q, parity, pl.ds(pl.multiple_of(part * MAJOR + 8 * block, 8), 8), across]
                        for part in range(2)
                    )

                even = dft16(functools.partial(load, 0))
                odd = dft16(functools.partial(load, 1))
                for n1 in range(16):
                    k = n1 - 8
                    value = plus(even[k % 16], times(odd[k % 16], k, 32))
                    for part in range(2):
                        tall[part, n1, pl.ds(pl.multiple_of(8 * block, 8), 8), :] = value[part]

            for part in range(2):
                @pl.loop(0, CUTS)
                def _(cut):
                    if unit:
                        leave(unit - 1, part, cut).wait()
                    for member in range(16 // CUTS):
                        n1 = cut * (16 // CUTS) + member
                        at = pl.ds(pl.multiple_of(n1 * LANES, LANES), LANES)
                        turned = jnp.transpose(tall[part, n1]) * scale_ref[pl.ds(0, 1), at]
                        for row in range(rows):
                            wide[part, row, :, at] = turned[row * bins : (row + 1) * bins]
                    leave(unit, part, cut).start()
        for part in range(2):
            for cut in range(CUTS):
                leave(count - 1, part, cut).wait()

    if close:
        begin()
        pl.loop(0, MINOR, unroll=2)(step)
        end_close()
    else:
        now = pl.program_id(0)
        pl.when(now == 0)(begin)
        pl.when(now < MINOR)(lambda: step(now))
        pl.when(now == MINOR)(end)


def finish(recv, weight, turn, scale, base, first, total):
    devices, count = recv.shape[0], recv.shape[1]
    bins = BINS // devices
    rows = LANES // bins
    _, entries = windows()
    close = count == 1
    if close:
        in_specs = [
            pl.BlockSpec(memory_space=pltpu.VMEM),
            pl.BlockSpec(memory_space=pl.ANY),
            pl.BlockSpec(memory_space=pl.ANY),
        ]
    else:
        in_specs = [
            pl.BlockSpec(recv.shape, lambda q: (0, 0, 0, 0, 0), pipeline_mode=pl.Buffered(1)),
            pl.BlockSpec((1, entries, 8, LANES), lambda q: (jnp.minimum(q, MINOR - 1), 0, 0, 0)),
            pl.BlockSpec((1, 2, 2, 2 * MAJOR, 2 * MAJOR), lambda q: (jnp.maximum(q - 1, 0), 0, 0, 0, 0)),
        ]
    in_specs.append(pl.BlockSpec((1, PULSES), (lambda: (0, 0)) if close else (lambda q: (0, 0))))
    args = [recv, weight, turn, scale]
    if base is not None:
        in_specs.append(pl.BlockSpec(memory_space=pl.ANY))
        args.append(base)
    ahead = []
    if close:
        ahead = [
            pltpu.VMEM(weight.shape, jnp.float32),
            pltpu.VMEM(turn.shape, jnp.bfloat16),
            pltpu.SemaphoreType.DMA((2, MINOR)),
        ]
    return pl.pallas_call(
        functools.partial(main_body, first, count, rows, bins, base is not None, close),
        grid=() if close else (MINOR + 1,),
        in_specs=in_specs,
        out_specs=pl.BlockSpec(memory_space=pl.ANY),
        out_shape=jax.ShapeDtypeStruct((2, total, bins, PULSES), jnp.float32),
        scratch_shapes=[
            pltpu.VMEM((MINOR + 2 * PAD, 2, count, MAJOR, LANES), jnp.float32),
            pltpu.VMEM((2, 2 * MAJOR, count * LANES), jnp.float32),
            pltpu.VMEM((MINOR, 2) + ((LANES, 2 * MAJOR) if close else (2 * MAJOR, count * LANES)), jnp.float32),
            pltpu.VMEM((2, 16, MAJOR, LANES), jnp.float32),
            pltpu.VMEM((2, rows, bins, PULSES), jnp.float32),
            pltpu.SemaphoreType.DMA((count, 2, CUTS)),
        ]
        + ahead,
        input_output_aliases={} if base is None else {4: 0},
        compiler_params=pltpu.CompilerParams(vmem_limit_bytes=(48 if close else 58) * 2**20),
        cost_estimate=pl.CostEstimate(
            flops=count * 32 * 6 * 256 * 256 * 128, bytes_accessed=(36 + 4 * count) * 2**20, transcendentals=0
        ),
        name="finish",
    )(*args)


def on_device(devices, echo, spectral_shift_units):
    bins = BINS // devices
    rows = LANES // bins
    lead = echo.shape[1] * echo.shape[2]
    flat = echo.reshape((2, lead) + echo.shape[3:])
    units = lead // rows
    cuts = (0, units - 1, units) if units > 1 else (0, units)
    codes = lax.dynamic_slice_in_dim(spectral_shift_units, lax.axis_index("pulse") * bins, bins, 0)
    sent = [pack(flat, first, last - first, devices) for first, last in zip(cuts[:-1], cuts[1:])]
    weight = weights(jnp.tile(codes, rows), bins)
    received = [lax.all_to_all(sent[0], "pulse", 0, 0, tiled=True)]
    for later in sent[1:]:
        later, weight = lax.optimization_barrier((later, weight))
        received.append(lax.all_to_all(later, "pulse", 0, 0, tiled=True))
    turn = jnp.asarray(turns())
    scale = correction(PULSES).reshape(1, PULSES)
    out = None
    for first, recv in zip(cuts[:-1], received):
        out = finish(recv, weight, turn, scale, out, first, lead)
    return out.reshape(echo.shape[:3] + (bins, PULSES))


def solution(mesh):
    placed = (P(None, "grp", None, "pulse", None), P())
    return jax.shard_map(
        functools.partial(on_device, mesh.shape["pulse"]),
        mesh=mesh,
        in_specs=placed,
        out_specs=P(None, "grp", None, "pulse", None),
        check_vma=False,
    )
```
